512 devices in a mesh: expert: 8 (over x, core), hidden: 64 (over y, z).
Axes of the slice: x: 4, y: 8, z: 8, core: 2. Of those that a mesh axis runs over, the one named last changes fastest.
Arguments:
- tokens: bfloat16 [1024, 3072], P('expert', 'hidden'), may hold values from -6 to 6
- grad_out: bfloat16 [1024, 3072], P('expert', 'hidden'), may hold values from -6 to 6
- lang_ids: int32 [1024, 1], P('expert'), may hold values from 0 to 7; in each aligned block of 128 rows (0 to 127, 128 to 255, ...) at most 40 rows name the same one
- gate_weight: bfloat16 [8, 3072, 8192], P('expert', None, 'hidden'), may hold values from -0.3125 to 0.3125
- up_weight: bfloat16 [8, 3072, 8192], P('expert', None, 'hidden'), may hold values from -0.109375 to 0.109375
- down_weight: bfloat16 [8, 8192, 3072], P('expert', 'hidden'), may hold values from -0.0625 to 0.0625
Outputs:
- grad_tokens: bfloat16 [1024, 3072], P('expert', 'hidden')
- grad_gate: bfloat16 [8, 3072, 8192], P('expert', None, 'hidden')
- grad_up: bfloat16 [8, 3072, 8192], P('expert', None, 'hidden')
- grad_down: bfloat16 [8, 8192, 3072], P('expert', 'hidden')
The draws below stay inside these ranges and needn't reach their ends.
Inputs may be any that keep to these rules, and one draw needn't show every extreme that they name: `lang_ids`: in each aligned block of 128 tokens at most 40 tokens name one expert; some block reaches 40. Every expert is named by some token.
All inputs are finite; a program needn't handle non-finite values.
Results may differ from the reference program's by a relative error of at most 0.005.
Values may be sent and summed in bfloat16 or wider, within the bound.
A program may use at most 64 MiB of HBM per device.

```python
import math
import jax
import jax.numpy as jnp
import numpy as np
from jax import lax

D = 3072
FF = 8192
TOK_DEV = 128
EXPERTS = 8
TOKENS = 1024
CAP = 40


def spiked(array, stream_key, source, target, parts, factor):
    owner, partner = [(jnp.arange(array.shape[dim]) // (array.shape[dim] // parts)).reshape([-1 if axis == dim else 1 for axis in range(array.ndim)]) for dim in (source, target)]
    chosen = jax.random.permutation(stream_key, parts)[partner]
    strong = (owner == chosen) | (owner == (partner + parts // 2) % parts)
    return jnp.where(strong, factor * array, array)


def block_scale(stream_key, dims, split, low, high):
    factor_of = 1.0
    for dim, parts in split:
        steps = jax.random.uniform(jax.random.fold_in(jax.random.fold_in(stream_key, 6), dim), (parts,), jnp.float32, low / len(split), high / len(split))
        factor_of = factor_of * jnp.repeat(jnp.exp(steps), dims[dim] // parts).reshape((-1,) + (1,) * (len(dims) - 1 - dim))
    return factor_of


def routed_block(rng, own, number, rows, amount, top, bound, skew):
    ranking = jax.random.permutation(rng, amount)
    crowded, ordinary = load_shares(amount, rows * top, bound, skew, True), load_shares(amount, rows * top, bound, skew, False)
    places = jnp.arange(amount)

    def named(sizes, rotation):
        used = int((sizes > 0).sum())
        fixed = max(1, used // 4)
        moved = fixed + (places - fixed + rotation * (used - fixed)) % max(1, amount - fixed)
        return jnp.zeros((amount,), jnp.int32).at[ranking[jnp.where(places < fixed, places, moved)]].set(jnp.asarray(sizes, jnp.int32))

    sizes = jnp.where(number % 4 == 0, named(crowded, number // 4), named(ordinary, number - number // 4 - 1))
    mixed = jax.random.permutation(jax.random.fold_in(own, 3), amount)
    donor, sink = mixed[0:amount // 2 * 2:2], mixed[1:amount // 2 * 2:2]
    room = jnp.minimum(sizes[donor] - 1, bound - sizes[sink]) // 2
    room = jnp.where((donor == ranking[0]) | (sink == ranking[0]) | (sizes[sink] == 0), 0, jnp.maximum(room, 0))
    moved = jax.random.randint(jax.random.fold_in(own, 4), (amount // 2,), 0, 1 << 20) % (room + 1)
    sizes = sizes.at[donor].add(-moved).at[sink].add(moved)
    labels = jnp.searchsorted(jnp.cumsum(sizes), jnp.arange(rows * top), side="right").astype(jnp.int32)
    table = labels.reshape(top, rows).T
    table = table[jax.random.permutation(jax.random.fold_in(own, 1), rows)]
    rotation = jax.random.randint(jax.random.fold_in(own, 2), (rows, 1), 0, top)
    return jnp.take_along_axis(table, (jnp.arange(top)[None, :] + rotation) % top, axis=1)


def load_shares(number_of, total, limit, slope, full):
    portions = [(1 << 20) // math.isqrt(rank ** slope) + 1 for rank in range(1, number_of + 1)]
    largest = limit if full else min(limit, max(-(-total // number_of), total * portions[0] // sum(portions)))
    least = 1 if total - largest >= number_of - 1 else 0
    counts, rest = [largest] + [least] * (number_of - 1), total - largest - least * (number_of - 1)
    while rest > 0:
        movable = [i for i in range(1, number_of) if counts[i] < largest] or [i for i in range(1, number_of) if counts[i] < limit]
        mass, remaining = sum([portions[i] for i in movable]), rest
        for i in movable:
            extra = min(limit - counts[i], max(1, remaining * portions[i] // mass), rest)
            counts[i] = counts[i] + extra
            rest = rest - extra
    return np.array(counts)


def scatter_about(own_key, shape, width, reach, cuts=(), kind=jnp.bfloat16):
    drawn = width * jax.random.normal(own_key, shape, jnp.float32)
    if cuts:
        drawn = drawn * block_scale(own_key, shape, cuts, -0.22, 0.18)
    return jnp.clip(drawn, -reach, reach).astype(kind)


def heavy_noise(stream_key, shape, width, most, shards, heavy, kind=jnp.bfloat16):
    values = width * jax.random.normal(stream_key, shape, jnp.float32)
    if shards:
        values = values * block_scale(stream_key, shape, shards, -0.22, 0.18)
    return jnp.clip(spiked(values, jax.random.fold_in(stream_key, 3), *heavy), -most, most).astype(kind)


def setup_inputs(seed: int = 0) -> dict:
    key_of = jax.random.split(jax.random.key(seed), 7)
    tokens = scatter_about(key_of[0], (TOKENS, D), 1.0, 6.0, ((0, 8), (1, 64)))
    grad_out = scatter_about(key_of[1], (TOKENS, D), 1.0, 6.0, ((0, 8), (1, 64)))
    lang_ids_keys = jax.random.split(jax.random.fold_in(key_of[2], 1), TOKENS // TOK_DEV)
    lang_ids_turns = jax.random.permutation(jax.random.fold_in(key_of[2], 3), TOKENS // TOK_DEV)
    lang_ids = jax.vmap(lambda own, number: routed_block(jax.random.fold_in(key_of[2], 2), own, number, TOK_DEV, EXPERTS, 1, CAP, 2))(lang_ids_keys, lang_ids_turns).reshape((TOKENS, 1))
    gate_weight = heavy_noise(key_of[3], (EXPERTS, D, FF), D ** -0.5, 0.3125, ((0, 8), (2, 64)), (2, 1, 64, 4.0))
    up_weight = scatter_about(key_of[4], (EXPERTS, D, FF), D ** -0.5, 0.109375, ((0, 8), (2, 64)))
    down_weight = scatter_about(key_of[5], (EXPERTS, FF, D), FF ** -0.5, 0.0625, ((0, 8), (1, 64)))
    return {"tokens": tokens, "grad_out": grad_out, "lang_ids": lang_ids, "gate_weight": gate_weight, "up_weight": up_weight, "down_weight": down_weight}


def contract_rows(left, right):
    return lax.dot_general(left, right, (((0,), (0,)), ((), ())), preferred_element_type=jnp.float32)


def contract_cols(left, right):
    return lax.dot_general(left, right, (((1,), (1,)), ((), ())), preferred_element_type=jnp.float32)


def slot_index(expert_ids, count):
    onehot = (expert_ids[:, None] == jnp.arange(count, dtype=jnp.int32)[None, :]).astype(jnp.int32)
    before = jnp.cumsum(onehot, axis=0) - onehot
    return jnp.sum(before * onehot, axis=1).astype(jnp.int32)


def expert_backward(x_rows, dy_rows, w_gate, w_up, w_down):
    gate_pre = jnp.dot(x_rows, w_gate, preferred_element_type=jnp.float32)
    up_pre = jnp.dot(x_rows, w_up, preferred_element_type=jnp.float32)
    sigma_gate = jax.nn.sigmoid(gate_pre)
    activated = gate_pre * sigma_gate
    hidden = (activated * up_pre).astype(jnp.bfloat16)
    d_hidden = contract_cols(dy_rows, w_down)
    d_up = (d_hidden * activated).astype(jnp.bfloat16)
    d_gate = (d_hidden * up_pre * sigma_gate * (1.0 + gate_pre * (1.0 - sigma_gate))).astype(jnp.bfloat16)
    grad_gate = contract_rows(x_rows, d_gate).astype(jnp.bfloat16)
    grad_up = contract_rows(x_rows, d_up).astype(jnp.bfloat16)
    grad_down = contract_rows(hidden, dy_rows).astype(jnp.bfloat16)
    partial_sum = contract_cols(d_gate, w_gate) + contract_cols(d_up, w_up)
    return grad_gate, grad_up, grad_down, partial_sum


def per_expert(packed):
    grad_gate, grad_up, grad_down, partial_sum = expert_backward(packed[0], packed[1], packed[2], packed[3], packed[4])
    return grad_gate, grad_up, grad_down, partial_sum.astype(jnp.bfloat16)


def partial_slots(block):
    return slot_index(block, EXPERTS)


def reference(tokens, grad_out, lang_ids, gate_weight, up_weight, down_weight):
    expert_ids = lang_ids[:, 0].astype(jnp.int32)
    blocks = expert_ids.reshape(EXPERTS, TOK_DEV)
    slots = jax.vmap(partial_slots)(blocks).reshape(TOKENS)
    block_of = jnp.arange(TOKENS, dtype=jnp.int32) // TOK_DEV
    position = (block_of * CAP + slots).astype(jnp.int32)
    empty = jnp.zeros((EXPERTS, EXPERTS * CAP, D), jnp.bfloat16)
    x_buffer = empty.at[expert_ids, position].set(tokens)
    dy_buffer = empty.at[expert_ids, position].set(grad_out)
    grad_gate, grad_up, grad_down, back_rows = lax.map(per_expert, (x_buffer, dy_buffer, gate_weight, up_weight, down_weight))
    grad_tokens = back_rows[expert_ids, position]
    return grad_tokens, grad_gate, grad_up, grad_down
```

```python
import jax
import jax.numpy as jnp
from jax import lax
from jax.experimental import pallas as pl
from jax.experimental.pallas import tpu as pltpu
from jax.sharding import PartitionSpec as P

MESH = pl.DeviceIdType.MESH
BF16 = jnp.bfloat16
F32 = jnp.float32

N = 8
CAP = 40
CHUNK = 48
HID = 128
D = 64 * CHUNK
MAIN = 256
XD = 640
DR = 384


def tn(left, right):
    return lax.dot_general(left, right, (((0,), (0,)), ((), ())), preferred_element_type=F32)


def nt(left, right):
    return lax.dot_general(left, right, (((1,), (1,)), ((), ())), preferred_element_type=F32)


def nn(left, right):
    return lax.dot_general(left, right, (((1,), (0,)), ((), ())), preferred_element_type=F32)


def iota(shape, dim):
    return lax.broadcasted_iota(jnp.int32, shape, dim)


def hops(i, right):
    return 4 if (i % 2 == 0) == right else 3


def kernel(
    x_ref, dy_ref, lang_ref, wg_hbm, wu_hbm, wd_hbm,
    gt_ref, gg_hbm, gu_hbm, gd_hbm,
    wg, wu, wd, wdt, msg, blk, xd, place, oht, acc_gu, acc_d, acc_t, gcat, hcat,
    part, rsend, rrecv, ssend, srecv, bsend, brecv, gg, gu, gd,
    wsem, a_s, a_r, m_s, m_r, g_s, g_r, r_s, r_r, s_s, s_r, b_s, b_r, osem,
):
    e = lax.axis_index("expert")
    hid = lax.axis_index("hidden")
    core = lax.rem(e, 2)
    y, z = hid // N, lax.rem(hid, N)
    a = y * (1 - core) + z * core
    b = z * (1 - core) + y * core
    sa, sb = N - 7 * core, 1 + 7 * core

    def wrap(v):
        return lax.rem(v + 2 * N, N)

    def hx(aa, bb):
        return aa * sa + bb * sb

    def rows(h):
        return pl.ds(pl.multiple_of(h * CHUNK, CHUNK), CHUNK)

    def remote(src, dst, ss, rs, dev):
        return pltpu.make_async_remote_copy(
            src_ref=src, dst_ref=dst, send_sem=ss, recv_sem=rs, device_id=dev, device_id_type=MESH
        )

    bar = pltpu.get_barrier_semaphore()
    for j in range(1, N):
        pl.semaphore_signal(bar, inc=1, device_id={"expert": wrap(e + j)}, device_id_type=MESH)
        pl.semaphore_signal(bar, inc=1, device_id={"hidden": hx(wrap(a + j), b)}, device_id_type=MESH)
    for d in (1, -1):
        pl.semaphore_signal(bar, inc=1, device_id={"hidden": hx(a, wrap(b + d))}, device_id_type=MESH)

    loads = [
        pltpu.make_async_copy(src, dst, wsem.at[k])
        for k, (src, dst) in enumerate(((wg_hbm, wg), (wu_hbm, wu), (wd_hbm, wd)))
    ]
    for c in loads:
        c.start()

    lang = lang_ref[...]
    member = iota((N, 128), 0) == lang
    earlier = (iota((128, 128), 0) < iota((128, 128), 1)).astype(BF16)
    before = nn(member.astype(BF16), earlier)
    slot = jnp.sum(jnp.where(member, before, 0.0), axis=0, keepdims=True).astype(jnp.int32)
    row = lang * 128 + slot
    line = iota((N * 128, 128), 0)
    oht[:, 0:128] = (line == row).astype(BF16)
    oht[:, 128:256] = (line == row + 64).astype(BF16)
    both = jnp.concatenate([x_ref[...], dy_ref[...]], axis=1)
    out = nt(both, oht[...]).astype(BF16)
    for k in range(N):
        msg[k] = out[:, k * 128 : (k + 1) * 128]

    pl.semaphore_wait(bar, 2 * (N - 1) + 2)

    def to_expert(j, src, dst, ss, rs):
        return remote(src.at[wrap(e + j)], dst.at[e], ss.at[j], rs.at[j], {"expert": wrap(e + j)})

    a2a = [to_expert(j, msg, blk, a_s, a_r) for j in range(1, N)]
    for c in a2a:
        c.start()
    blk[e] = msg[e]

    r1 = iota((N * 128, 1), 0)
    blk_i, j_i = r1 // 128, lax.rem(r1, 128)
    is_dy = j_i >= 64
    jj = jnp.where(is_dy, j_i - 64, j_i)
    pos = blk_i * CAP + jj
    lane = jnp.where(
        pos < MAIN, pos + jnp.where(is_dy, MAIN, 0), pos + jnp.where(is_dy, 2 * MAIN - MAIN + 64, 2 * MAIN - MAIN)
    )
    lane = jnp.where(jj < CAP, lane, -1)
    place[...] = (iota((N * 128, XD), 1) == lane).astype(BF16)

    for c in loads:
        c.wait()
    for k in range(D // 128):
        wdt[pl.ds(k * 128, 128), :] = wd[:, k * 128 : (k + 1) * 128].T
    acc_gu[...] = jnp.zeros_like(acc_gu)
    acc_d[...] = jnp.zeros_like(acc_d)
    acc_t[...] = jnp.zeros_like(acc_t)

    for c in a2a:
        c.wait()
    cat = jnp.concatenate([blk[k] for k in range(N)], axis=1)
    xd[hid] = nn(cat, place[...]).astype(BF16)

    def small(k, chunk, to):
        h = hx(wrap(a + chunk), b)
        return remote(xd.at[h], xd.at[h], m_s.at[k], m_r.at[k], {"hidden": hx(wrap(a + to), b)})

    def big(i, off, right, s):
        k, d = (0, 1) if right else (1, -1)
        h = hx(wrap(a + off), wrap(b - d * s))
        return remote(
            xd.at[h], xd.at[h], g_s.at[k, i, s], g_r.at[k, i, s], {"hidden": hx(a, wrap(b + d))}
        )

    def big_recv(i, off, right, s):
        k, d = (0, 1) if right else (1, -1)
        h = hx(wrap(a + off), wrap(b - d * (s + 1)))
        return remote(
            xd.at[h], xd.at[h], g_s.at[k, i, s], g_r.at[k, i, s], {"hidden": hx(a, wrap(b + d))}
        )

    def small_recv(k):
        small(k, k, 0).wait_recv()

    def offset(i2, p):
        return -i2 if p == 0 else i2 + 1

    def send_big(i, off, s, parity=None):
        for right in (True, False):
            if s < hops(i if parity is None else parity, right):
                if s > 0:
                    big_recv(i, off, right, s - 1).wait_recv()
                big(i, off, right, s).start()

    even = lax.rem(a, 2)
    far = 2 - 4 * even
    sends = [small(1, 0, -1), small(7, 0, 1), small(2, 0, -2), small(6, 0, 2)]
    sends[0].start()
    sends[1].start()
    send_big(0, 0, 0)
    sends[2].start()
    sends[3].start()
    small_recv(1)
    send_big(1, 1, 0)
    small_recv(7)
    send_big(2, -1, 0)
    small_recv(2)
    relay = [small(3, 2, -1), small(5, -2, 1), small(4, far, -far)]
    relay[0].start()
    small_recv(6)
    relay[1].start()
    relay[2].start()
    send_big(3, 2, 0)
    send_big(4, -2, 0)
    send_big(0, 0, 1)
    small_recv(3)
    send_big(5, 3, 0)
    small_recv(5)
    send_big(6, -3, 0)
    small_recv(4)
    send_big(7, 4, 0)

    def column(ref, dist):
        o = wrap(b + dist)
        return [hx(wrap(a + r), o) for r in range(N)]

    def forward(dist):
        hs = column(xd, dist)
        left = jnp.concatenate(
            [jnp.concatenate([wg[rows(h), :], wu[rows(h), :], wdt[rows(h), :]], axis=1) for h in hs], axis=0
        )
        right = jnp.concatenate([xd[h] for h in hs], axis=0)
        acc_gu[...] += tn(left[:, 0 : 2 * HID], right[:, 0:MAIN])
        acc_d[...] += tn(left[:, 2 * HID : 3 * HID], right[:, MAIN : 2 * MAIN])
        acc_t[...] += tn(left, right[:, 2 * MAIN : XD])

    forward(0)
    for s in range(1, 4):
        def step(i2, carry):
            for p in (0, 1):
                send_big(2 * i2 + p, offset(i2, p), s, p)
            return carry

        if s == 1:
            send_big(1, 1, 1)
            lax.fori_loop(1, 4, step, 0)
        else:
            lax.fori_loop(0, 4, step, 0)

        if s == 3:
            def last(i2, carry):
                for p in (0, 1):
                    for right in (True, False):
                        if hops(p, right) == 3:
                            big_recv(2 * i2 + p, offset(i2, p), right, 2).wait_recv()
                return carry

            lax.fori_loop(0, 4, last, 0)

        def two(k, carry):
            forward((1 - 2 * k) * s)
            return carry

        lax.fori_loop(0, 2, two, 0)

    def end(i2, carry):
        for p in (0, 1):
            for right in (True, False):
                if hops(p, right) == 4:
                    big_recv(2 * i2 + p, offset(i2, p), right, 3).wait_recv()
        return carry

    lax.fori_loop(0, 4, end, 0)
    forward(4)

    def units(gate, up, dh):
        sig = jax.nn.sigmoid(gate)
        act = gate * sig
        return (
            (act * up).astype(BF16),
            (dh * up * sig * (1.0 + gate * (1.0 - sig))).astype(BF16),
            (dh * act).astype(BF16),
        )

    h_m, g_m, u_m = units(acc_gu[0:HID, :], acc_gu[HID : 2 * HID, :], acc_d[...])
    tail = acc_t[...]
    dh_t = pltpu.roll(tail[2 * HID : 3 * HID, :], 64, 1)
    h_t, g_t, u_t = units(tail[0:HID, :], tail[HID : 2 * HID, :], dh_t)
    low = iota((HID, 128), 1) < 64
    zero = jnp.zeros((HID, 128), BF16)
    gcat[0:HID, 0:MAIN] = g_m
    gcat[HID : 2 * HID, 0:MAIN] = u_m
    gcat[0:HID, MAIN:DR] = jnp.where(low, g_t, zero)
    gcat[HID : 2 * HID, MAIN:DR] = jnp.where(low, u_t, zero)
    hcat[:, 0:MAIN] = h_m
    h_shift = pltpu.roll(h_t.astype(F32), 64, 1).astype(BF16)
    hcat[:, MAIN:DR] = jnp.where(low, zero, h_shift)

    def partial_sums(dist):
        hs = column(part, dist)
        left = jnp.concatenate(
            [jnp.concatenate([wg[rows(h), :], wu[rows(h), :]], axis=1) for h in hs], axis=0
        )
        part[dist % N] = nn(left, gcat[...]).reshape(N, CHUNK, DR)

    def reduce_copy(i, right, s):
        k, d = (0, 1) if right else (1, -1)
        return remote(
            rsend.at[k, i, s], rrecv.at[k, i, s], r_s.at[k, i, s], r_r.at[k, i, s], {"hidden": hx(a, wrap(b + d))}
        )

    def reduce_step(i, p, right, s):
        k, d = (0, 1) if right else (1, -1)
        far_off = d * (hops(p, right) - s)
        value = part[far_off % N, i]
        if s > 0:
            reduce_copy(i, right, s - 1).wait_recv()
            value = value + rrecv[k, i, s - 1].astype(F32)
        rsend[k, i, s] = value.astype(BF16)
        reduce_copy(i, right, s).start()

    def reduce_stage(s, pick):
        def step(i2, carry):
            for p in (0, 1):
                for right in (True, False):
                    if s < hops(p, right) and hops(p, right) in pick:
                        reduce_step(2 * i2 + p, p, right, s)
            return carry

        lax.fori_loop(0, 4, step, 0)

    outs = []

    def weight_grads(g):
        first = g * N * CHUNK
        span = pl.ds(pl.multiple_of(first, N * CHUNK), N * CHUNK)
        feat = xd[pl.ds(g * N, N)].reshape(N * CHUNK, XD)
        x_rows = jnp.concatenate([feat[:, 0:MAIN], feat[:, 2 * MAIN : XD]], axis=1)
        dy_rows = feat[:, MAIN:XD]
        pair = nt(x_rows, gcat[...]).astype(BF16)
        gg[span, :] = pair[:, 0:HID]
        gu[span, :] = pair[:, HID : 2 * HID]
        gd[:, span] = nt(hcat[...], dy_rows).astype(BF16)
        for k, (src, dst) in enumerate(((gg, gg_hbm), (gu, gu_hbm))):
            pltpu.make_async_copy(src.at[span, :], dst.at[span, :], osem.at[k, g]).start()
        pltpu.make_async_copy(gd.at[:, span], gd_hbm.at[:, span], osem.at[2, g]).start()

    def grads(lo, hi):
        def one(g, carry):
            weight_grads(g)
            return carry

        lax.fori_loop(lo, hi, one, 0)

    partial_sums(4)
    reduce_stage(0, (4,))
    partial_sums(3)
    partial_sums(-3)
    reduce_stage(0, (3,))
    for dist in (2, -2, 1, -1, 0):
        partial_sums(dist)
    reduce_stage(1, (3, 4))
    grads(0, 2)
    reduce_stage(2, (3, 4))
    grads(2, 5)
    reduce_stage(3, (3, 4))
    grads(5, 8)

    def collect(i, p):
        value = part[0, i]
        for right in (True, False):
            k, s = (0 if right else 1), hops(p, right) - 1
            reduce_copy(i, right, s).wait_recv()
            value = value + rrecv[k, i, s].astype(F32)
        return value

    def small_sum(i):
        return remote(
            ssend.at[i], srecv.at[i], s_s.at[i], s_r.at[i], {"hidden": hx(wrap(a + i), b)}
        )

    for i in (4, 3, 5, 2, 6, 1, 7):
        ssend[i] = collect(i, i % 2).astype(BF16)
        small_sum(i).start()
    total = collect(0, 0)

    p_i = iota((DR, N * 128), 0)
    c_i = iota((DR, N * 128), 1)
    j_c = lax.rem(c_i, 128)
    pick = ((p_i == (c_i // 128) * CAP + j_c) & (j_c < CAP)).astype(BF16)

    for i in (1, 7, 2, 6, 3, 5, 4):
        small_sum(i).wait_recv()
        total = total + srecv[i].astype(F32)
    back = nn(total.astype(BF16), pick).astype(BF16)
    for k in range(N):
        bsend[k] = back[:, k * 128 : (k + 1) * 128]
    home = [to_expert(j, bsend, brecv, b_s, b_r) for j in range(1, N)]
    for c in home:
        c.start()
    brecv[e] = bsend[e]

    for c in sends + relay:
        c.wait_send()

    def close(i2, carry):
        for p in (0, 1):
            for right in (True, False):
                for s in range(hops(p, right)):
                    big(2 * i2 + p, offset(i2, p), right, s).wait_send()
                    reduce_copy(2 * i2 + p, right, s).wait_send()
        return carry

    lax.fori_loop(0, 4, close, 0)
    for i in range(1, N):
        small_sum(i).wait_send()

    def flush(g, carry):
        span = pl.ds(pl.multiple_of(g * N * CHUNK, N * CHUNK), N * CHUNK)
        for k, (src, dst) in enumerate(((gg, gg_hbm), (gu, gu_hbm))):
            pltpu.make_async_copy(src.at[span, :], dst.at[span, :], osem.at[k, g]).wait()
        pltpu.make_async_copy(gd.at[:, span], gd_hbm.at[:, span], osem.at[2, g]).wait()
        return carry

    lax.fori_loop(0, N, flush, 0)

    for c in home:
        c.wait()
    cat = jnp.concatenate([brecv[k] for k in range(N)], axis=1)
    gt_ref[...] = nn(cat, oht[:, 0:128]).astype(BF16)


def local(tokens, grad_out, lang_ids, gate_weight, up_weight, down_weight):
    vmem = pl.BlockSpec(memory_space=pltpu.VMEM)
    anyspace = pl.BlockSpec(memory_space=pl.ANY)
    dma = pltpu.SemaphoreType.DMA
    scratch = [
        pltpu.VMEM((D, HID), BF16),
        pltpu.VMEM((D, HID), BF16),
        pltpu.VMEM((HID, D), BF16),
        pltpu.VMEM((D, HID), BF16),
        pltpu.VMEM((N, CHUNK, 128), BF16),
        pltpu.VMEM((N, CHUNK, 128), BF16),
        pltpu.VMEM((64, CHUNK, XD), BF16),
        pltpu.VMEM((N * 128, XD), BF16),
        pltpu.VMEM((N * 128, 256), BF16),
        pltpu.VMEM((2 * HID, MAIN), F32),
        pltpu.VMEM((HID, MAIN), F32),
        pltpu.VMEM((3 * HID, 128), F32),
        pltpu.VMEM((2 * HID, DR), BF16),
        pltpu.VMEM((HID, DR), BF16),
        pltpu.VMEM((N, N, CHUNK, DR), F32),
        pltpu.VMEM((2, N, 4, CHUNK, DR), BF16),
        pltpu.VMEM((2, N, 4, CHUNK, DR), BF16),
        pltpu.VMEM((N, CHUNK, DR), BF16),
        pltpu.VMEM((N, CHUNK, DR), BF16),
        pltpu.VMEM((N, CHUNK, 128), BF16),
        pltpu.VMEM((N, CHUNK, 128), BF16),
        pltpu.VMEM((D, HID), BF16),
        pltpu.VMEM((D, HID), BF16),
        pltpu.VMEM((HID, D), BF16),
        dma((3,)),
        dma((N,)), dma((N,)),
        dma((N,)), dma((N,)),
        dma((2, N, 4)), dma((2, N, 4)),
        dma((2, N, 4)), dma((2, N, 4)),
        dma((N,)), dma((N,)),
        dma((N,)), dma((N,)),
        dma((3, N)),
    ]
    out = pl.pallas_call(
        kernel,
        out_shape=(
            jax.ShapeDtypeStruct((CHUNK, 128), BF16),
            jax.ShapeDtypeStruct((D, HID), BF16),
            jax.ShapeDtypeStruct((D, HID), BF16),
            jax.ShapeDtypeStruct((HID, D), BF16),
        ),
        in_specs=[vmem, vmem, vmem, anyspace, anyspace, anyspace],
        out_specs=(vmem, anyspace, anyspace, anyspace),
        scratch_shapes=scratch,
        compiler_params=pltpu.CompilerParams(
            collective_id=0, has_side_effects=True, vmem_limit_bytes=56 * 1024 * 1024
        ),
        cost_estimate=pl.CostEstimate(
            flops=16 * 320 * D * HID, bytes_accessed=6 * D * HID * 2, transcendentals=320 * HID
        ),
    )(
        tokens.T, grad_out.T, lang_ids.T, gate_weight[0], up_weight[0], down_weight[0]
    )
    return out[0].T, out[1][None], out[2][None], out[3][None]


def solution(mesh):
    in_specs = (
        P("expert", "hidden"),
        P("expert", "hidden"),
        P("expert", None),
        P("expert", None, "hidden"),
        P("expert", None, "hidden"),
        P("expert", "hidden", None),
    )
    out_specs = (
        P("expert", "hidden"),
        P("expert", None, "hidden"),
        P("expert", None, "hidden"),
        P("expert", "hidden", None),
    )
    return jax.shard_map(local, mesh=mesh, in_specs=in_specs, out_specs=out_specs, check_vma=False)
```

```python
import jax
import jax.numpy as jnp
from jax import lax
from jax.experimental import pallas as pl
from jax.experimental.pallas import tpu as pltpu
from jax.sharding import PartitionSpec as P

MESH = pl.DeviceIdType.MESH
BF16 = jnp.bfloat16
F32 = jnp.float32

N = 8
CAP = 40
CHUNK = 48
HID = 128
D = 64 * CHUNK
MAIN = 256
XD = 640
DR = 384


def tn(left, right):
    return lax.dot_general(left, right, (((0,), (0,)), ((), ())), preferred_element_type=F32)


def nt(left, right):
    return lax.dot_general(left, right, (((1,), (1,)), ((), ())), preferred_element_type=F32)


def nn(left, right):
    return lax.dot_general(left, right, (((1,), (0,)), ((), ())), preferred_element_type=F32)


def iota(shape, dim):
    return lax.broadcasted_iota(jnp.int32, shape, dim)


def off(i, odd):
    return 2 * i - 4 + odd


ORDER = (2, 1, 3, 0)
PEERS = (4, 3, 5, 2, 6, 1, 7)


def kernel(
    x_hbm, dy_hbm, lang_hbm, wg_hbm, wu_hbm, wd_hbm,
    gt_ref, gg_hbm, gu_hbm, gd_hbm,
    x_ref, dy_ref, lang_ref, wg, wu, wd, wdt, msg, blk, xd, place, oht, acc_gu, acc_d, acc_t, gcat, hcat,
    part, rsend, rrecv, ssend, srecv, bsend, brecv, gg, gu, gd,
    tsem, wsem, a_s, a_r, m_s, m_r, g_s, g_r, r_s, r_r, s_s, s_r, b_s, b_r, osem,
):
    tok = [
        pltpu.make_async_copy(src, dst, tsem.at[k])
        for k, (src, dst) in enumerate(((lang_hbm, lang_ref), (x_hbm, x_ref), (dy_hbm, dy_ref)))
    ]
    for c in tok:
        c.start()

    e = lax.axis_index("expert")
    hid = lax.axis_index("hidden")
    core = lax.rem(e, 2)
    y, z = hid // N, lax.rem(hid, N)
    own = lax.rem(y + z + core, 2)
    way = (own, 1 - own)

    def wrap(v):
        return lax.rem(v + 2 * N, N)

    def way_of(q):
        return lax.rem(own + q, 2)

    def first(q):
        c = way_of(q)
        return y * (1 - c) + z * c

    def hx(q, du, dv):
        c = way_of(q)
        u = wrap(y * (1 - c) + z * c + du)
        v = wrap(z * (1 - c) + y * c + dv)
        return u * (N - 7 * c) + v * (1 + 7 * c)

    def side(q, odd):
        return lax.rem((first(q) + odd) // 2, 2)

    def rows(h):
        return pl.ds(pl.multiple_of(h * CHUNK, CHUNK), CHUNK)

    def remote(src, dst, ss, rs, dev):
        return pltpu.make_async_remote_copy(
            src_ref=src, dst_ref=dst, send_sem=ss, recv_sem=rs, device_id=dev, device_id_type=MESH
        )

    bar = pltpu.get_barrier_semaphore()
    for j in range(1, N):
        pl.semaphore_signal(bar, inc=1, device_id={"expert": wrap(e + j)}, device_id_type=MESH)
        pl.semaphore_signal(bar, inc=1, device_id={"hidden": hx(0, j, 0)}, device_id_type=MESH)
    for j in (1, -1, 3, -3):
        pl.semaphore_signal(bar, inc=1, device_id={"hidden": hx(1, j, 0)}, device_id_type=MESH)

    loads = [
        pltpu.make_async_copy(src, dst, wsem.at[k])
        for k, (src, dst) in enumerate(((wg_hbm, wg), (wu_hbm, wu), (wd_hbm, wd)))
    ]
    for c in loads:
        c.start()
    for c in tok:
        c.wait()

    lang = lang_ref[...]
    member = iota((N, 128), 0) == lang
    earlier = (iota((128, 128), 0) < iota((128, 128), 1)).astype(BF16)
    before = nn(member.astype(BF16), earlier)
    slot = jnp.sum(jnp.where(member, before, 0.0), axis=0, keepdims=True).astype(jnp.int32)
    oht[...] = (iota((N * 64, 128), 0) == lang * 64 + slot).astype(BF16)
    out = nt(jnp.concatenate([x_ref[...], dy_ref[...]], axis=0), oht[...])
    low = iota((CHUNK, 128), 1) < 64
    for k in range(N):
        tile = slice(k // 2 * 128, k // 2 * 128 + 128)
        x_k, dy_k = out[0:CHUNK, tile], out[CHUNK : 2 * CHUNK, tile]
        if k % 2 == 0:
            dy_k = pltpu.roll(dy_k, 64, 1)
        else:
            x_k = pltpu.roll(x_k, 64, 1)
        msg[k] = jnp.where(low, x_k, dy_k).astype(BF16)

    pl.semaphore_wait(bar, 2 * (N - 1) + 4)

    def to_expert(j, src, dst, ss, rs):
        return remote(src.at[wrap(e + j)], dst.at[e], ss.at[j], rs.at[j], {"expert": wrap(e + j)})

    a2a = [to_expert(j, msg, blk, a_s, a_r) for j in PEERS]
    for c in a2a:
        c.start()
    blk[e] = msg[e]

    r1 = iota((N * 128, 1), 0)
    blk_i, j_i = r1 // 128, lax.rem(r1, 128)
    is_dy = j_i >= 64
    jj = jnp.where(is_dy, j_i - 64, j_i)
    pos = blk_i * CAP + jj
    lane = jnp.where(pos < MAIN, pos + jnp.where(is_dy, MAIN, 0), pos + jnp.where(is_dy, MAIN + 64, MAIN))
    lane = jnp.where(jj < CAP, lane, -1)
    place[...] = (iota((N * 128, XD), 1) == lane).astype(BF16)

    for c in loads:
        c.wait()
    for k in range(D // 128):
        wdt[pl.ds(k * 128, 128), :] = wd[:, k * 128 : (k + 1) * 128].T
    acc_gu[...] = jnp.zeros_like(acc_gu)
    acc_d[...] = jnp.zeros_like(acc_d)
    acc_t[...] = jnp.zeros_like(acc_t)

    for c in a2a:
        c.wait()
    cat = jnp.concatenate([blk[k] for k in range(N)], axis=1)
    xd[hid] = nn(cat, place[...]).astype(BF16)

    def small(k, q, chunk, to):
        h = hx(q, chunk, 0)
        return remote(xd.at[h], xd.at[h], m_s.at[k], m_r.at[k], {"hidden": hx(q, to, 0)})

    def small_recv(k):
        h = hx(k % 2, k, 0)
        remote(xd.at[h], xd.at[h], m_s.at[k], m_r.at[k], {"hidden": hid}).wait_recv()

    def big(q, i, d, s):
        to = 1 - 2 * d
        h = hx(q, off(i, (s + q) % 2), -to * s)
        c = way[q]
        return remote(
            xd.at[h], xd.at[h], g_s.at[c, d, s, i], g_r.at[c, d, s, i], {"hidden": hx(q, 0, to)}
        )

    def big_recv(q, i, d, s):
        to = 1 - 2 * d
        h = hx(q, off(i, (s + 1 + q) % 2), -to * (s + 1))
        c = way[q]
        remote(xd.at[h], xd.at[h], g_s.at[c, d, s, i], g_r.at[c, d, s, i], {"hidden": hid}).wait_recv()

    def goes_far(q, d, s):
        c = side(q, (s + q) % 2)
        c = c if d == 0 else 1 - c
        return [c, c + 2]

    def stays(q, d, s):
        c = side(q, (s + q) % 2)
        c = 1 - c if d == 0 else c
        return [c, c + 2]

    def send_big(q, i, s):
        for d in (0, 1):
            if s > 0:
                big_recv(q, i, d, s - 1)
            big(q, i, d, s).start()

    turn = side(0, 0)
    far = 2 - 4 * turn
    sends = [small(1, 0, 0, -1), small(7, 0, 0, 1), small(2, 0, 0, -2), small(6, 0, 0, 2)]
    relay = [small(3, 0, 2, -1), small(5, 0, -2, 1), small(4, 0, far, -far)]
    sends[0].start()
    sends[1].start()
    send_big(0, 2, 0)
    sends[2].start()
    sends[3].start()
    small_recv(1)
    send_big(1, 2, 0)
    small_recv(7)
    send_big(1, 1, 0)
    small_recv(2)
    relay[0].start()
    small_recv(6)
    relay[1].start()
    relay[2].start()
    send_big(0, 3, 0)
    send_big(0, 1, 0)
    send_big(1, 2, 1)
    small_recv(3)
    send_big(1, 3, 0)
    small_recv(5)
    send_big(1, 0, 0)
    small_recv(4)
    send_big(0, 0, 0)

    def forward(hs):
        left = jnp.concatenate(
            [jnp.concatenate([wg[rows(h), :], wu[rows(h), :], wdt[rows(h), :]], axis=1) for h in hs], axis=0
        )
        right = jnp.concatenate([xd[h] for h in hs], axis=0)
        acc_gu[...] += tn(left[:, 0 : 2 * HID], right[:, 0:MAIN])
        acc_d[...] += tn(left[:, 2 * HID : 3 * HID], right[:, MAIN : 2 * MAIN])
        acc_t[...] += tn(left, right[:, 2 * MAIN : XD])

    def column(dist):
        return [hx(q, off(i, (q + dist) % 2), dist) for q in (0, 1) for i in range(4)]

    forward(column(0))
    for s in range(1, 4):
        if s < 3:
            for i in ORDER:
                for q in (0, 1):
                    if (s, q, i) != (1, 1, 2):
                        send_big(q, i, s)
        else:
            for j in (0, 1):
                for q in (0, 1):
                    for d in (0, 1):
                        i = goes_far(q, d, 3)[j]
                        big_recv(q, i, d, 2)
                        big(q, i, d, 3).start()
            for q in (0, 1):
                for d in (0, 1):
                    for i in stays(q, d, 3):
                        big_recv(q, i, d, 2)

        def two(k, carry):
            forward(column((1 - 2 * k) * s))
            return carry

        lax.fori_loop(0, 2, two, 0)

    for q in (0, 1):
        for d in (0, 1):
            for i in goes_far(q, d, 4):
                big_recv(q, i, d, 3)
    forward(column(4))

    def units(gate, up, dh):
        sig = jax.nn.sigmoid(gate)
        act = gate * sig
        return (
            (act * up).astype(BF16),
            (dh * up * sig * (1.0 + gate * (1.0 - sig))).astype(BF16),
            (dh * act).astype(BF16),
        )

    h_m, g_m, u_m = units(acc_gu[0:HID, :], acc_gu[HID : 2 * HID, :], acc_d[...])
    tail = acc_t[...]
    dh_t = pltpu.roll(tail[2 * HID : 3 * HID, :], 64, 1)
    h_t, g_t, u_t = units(tail[0:HID, :], tail[HID : 2 * HID, :], dh_t)
    low_h = iota((HID, 128), 1) < 64
    for k, (m, t) in enumerate(((g_m, g_t), (u_m, u_t))):
        span = slice(k * HID, (k + 1) * HID)
        t = jnp.where(low_h, t.astype(F32), 0.0)
        gcat[span, 0:MAIN] = m
        gcat[span, MAIN:DR] = t.astype(BF16)
        gcat[span, DR : DR + 128] = pltpu.roll(t, 64, 1).astype(BF16)
    hcat[:, 0:MAIN] = h_m
    hcat[:, MAIN:DR] = pltpu.roll(jnp.where(low_h, h_t.astype(F32), 0.0), 64, 1).astype(BF16)

    def partial_sums(dist):
        hs = column(dist)
        left = jnp.concatenate(
            [jnp.concatenate([wg[rows(h), :], wu[rows(h), :]], axis=1) for h in hs], axis=0
        )
        res = nn(left, gcat[...])
        for n, h in enumerate(hs):
            block = res[n * CHUNK : (n + 1) * CHUNK]
            part[h, :, 0:MAIN] = block[:, 0:MAIN]
            part[h, :, MAIN:DR] = block[:, MAIN:DR] if n % 4 < 2 else block[:, DR : DR + 128]

    def reduce_copy(q, d, short, s):
        c = way[q]
        return remote(
            rsend.at[c, d, short, s],
            rrecv.at[c, d, short, s],
            r_s.at[c, d, short, s],
            r_r.at[c, d, short, s],
            {"hidden": hx(q, 0, 1 - 2 * d)},
        )

    def pair_parts(q, sel, odd, dist):
        h0, h1 = hx(q, off(sel, odd), dist), hx(q, off(sel + 2, odd), dist)
        return [part[h0, :, 0:MAIN], part[h1, :, 0:MAIN], part[h0, :, MAIN:DR] + part[h1, :, MAIN:DR]]

    def add_message(values, message):
        spans = ((0, MAIN), (MAIN, 2 * MAIN), (2 * MAIN, XD))
        return [v + message[:, lo:hi].astype(F32) for v, (lo, hi) in zip(values, spans)]

    def reduce_step(q, d, short, s):
        left_hops = 4 - short - s
        odd = (q + left_hops) % 2
        sel = side(q, odd)
        sel = sel if d == short else 1 - sel
        values = pair_parts(q, sel, odd, (1 - 2 * d) * left_hops)
        c = way[q]
        if s > 0:
            reduce_copy(q, d, short, s - 1).wait_recv()
            values = add_message(values, rrecv[c, d, short, s - 1])
        rsend[c, d, short, s] = jnp.concatenate([v.astype(BF16) for v in values], axis=1)
        reduce_copy(q, d, short, s).start()

    def reduce_stage(s, pick):
        for short in pick:
            for q in (0, 1):
                for d in (0, 1):
                    reduce_step(q, d, short, s)

    def weight_grads(g):
        span = pl.ds(pl.multiple_of(g * N * CHUNK, N * CHUNK), N * CHUNK)
        feat = xd[pl.ds(g * N, N)].reshape(N * CHUNK, XD)
        x_rows = jnp.concatenate([feat[:, 0:MAIN], feat[:, 2 * MAIN : XD]], axis=1)
        dy_rows = feat[:, MAIN:XD]
        pair = nt(x_rows, gcat[:, 0:DR]).astype(BF16)
        gg[span, :] = pair[:, 0:HID]
        gu[span, :] = pair[:, HID : 2 * HID]
        gd[:, span] = nt(hcat[...], dy_rows).astype(BF16)
        for k, (src, dst) in enumerate(((gg, gg_hbm), (gu, gu_hbm))):
            pltpu.make_async_copy(src.at[span, :], dst.at[span, :], osem.at[k, g]).start()
        pltpu.make_async_copy(gd.at[:, span], gd_hbm.at[:, span], osem.at[2, g]).start()

    def grads(lo, hi):
        def one(g, carry):
            weight_grads(g)
            return carry

        lax.fori_loop(lo, hi, one, 0)

    partial_sums(4)
    reduce_stage(0, (0,))
    partial_sums(3)
    partial_sums(-3)
    reduce_stage(0, (1,))

    def rest(k, carry):
        partial_sums(k - 2)
        return carry

    lax.fori_loop(0, 5, rest, 0)
    reduce_stage(1, (0, 1))
    grads(0, 3)
    reduce_stage(2, (0, 1))
    grads(3, 6)
    reduce_stage(3, (0,))
    grads(6, 8)

    def small_sum(k, q):
        return remote(ssend.at[k], srecv.at[k], s_s.at[k], s_r.at[k], {"hidden": hx(q, k, 0)})

    for q, sel in ((1, 0), (1, 1), (0, 1), (0, 0)):
        bit = lax.rem(side(q, q) + sel, 2)
        c = way[q]
        values = pair_parts(q, sel, q, 0)
        for d, short in ((0, bit), (1, 1 - bit)):
            last = 3 - short
            remote(
                rsend.at[c, d, short, last],
                rrecv.at[c, d, short, last],
                r_s.at[c, d, short, last],
                r_r.at[c, d, short, last],
                {"hidden": hid},
            ).wait_recv()
            values = add_message(values, rrecv[c, d, short, last])
        for j in (0, 1):
            k = off(sel + 2 * j, q) % N
            if k == 0:
                main, high = values[1], values[2]
            else:
                ssend[k] = jnp.concatenate([values[j].astype(BF16), values[2].astype(BF16)], axis=1)
                small_sum(k, q).start()
    low_sum = jnp.zeros((CHUNK, 128), F32)

    p_i = iota((DR, N * 128), 0)
    c_i = iota((DR, N * 128), 1)
    j_c = lax.rem(c_i, 128) - 64 * core
    pick = ((p_i == (c_i // 128) * CAP + j_c) & (j_c >= 0) & (j_c < CAP)).astype(BF16)

    for k in (1, 7, 2, 6, 3, 5, 4):
        remote(ssend.at[k], srecv.at[k], s_s.at[k], s_r.at[k], {"hidden": hid}).wait_recv()
        main = main + srecv[k, :, 0:MAIN].astype(F32)
        if k >= 4:
            low_sum = low_sum + srecv[k, :, MAIN:DR].astype(F32)
        else:
            high = high + srecv[k, :, MAIN:DR].astype(F32)
    tail = low_sum + pltpu.roll(high, 64, 1)
    total = jnp.concatenate([main.astype(BF16), tail.astype(BF16)], axis=1)
    back = nn(total, pick).astype(BF16)
    for k in range(N):
        bsend[k] = back[:, k * 128 : (k + 1) * 128]
    home = [to_expert(j, bsend, brecv, b_s, b_r) for j in PEERS]
    for c in home:
        c.start()
    brecv[e] = bsend[e]

    for c in sends + relay:
        c.wait_send()
    for q in (0, 1):
        for d in (0, 1):
            for s in range(3):
                for i in range(4):
                    big(q, i, d, s).wait_send()
            for i in goes_far(q, d, 3):
                big(q, i, d, 3).wait_send()
            for short in (0, 1):
                for s in range(4 - short):
                    reduce_copy(q, d, short, s).wait_send()
    for k in range(1, N):
        small_sum(k, k % 2).wait_send()

    def flush(g, carry):
        span = pl.ds(pl.multiple_of(g * N * CHUNK, N * CHUNK), N * CHUNK)
        for k, (src, dst) in enumerate(((gg, gg_hbm), (gu, gu_hbm))):
            pltpu.make_async_copy(src.at[span, :], dst.at[span, :], osem.at[k, g]).wait()
        pltpu.make_async_copy(gd.at[:, span], gd_hbm.at[:, span], osem.at[2, g]).wait()
        return carry

    lax.fori_loop(0, N, flush, 0)

    for c in home:
        c.wait()
    cat = jnp.concatenate([jnp.where(low, brecv[k], brecv[k + 1]) for k in range(0, N, 2)], axis=1)
    gt_ref[...] = nn(cat, oht[...]).astype(BF16)


def copy_kernel(gt, gg, gu, gd, gt_out, gg_out, gu_out, gd_out, sem):
    copies = [
        pltpu.make_async_copy(src, dst, sem.at[k])
        for k, (src, dst) in enumerate(((gg, gg_out), (gu, gu_out), (gd, gd_out)))
    ]
    for c in copies:
        c.start()
    gt_out[...] = gt[...]
    for c in copies:
        c.wait()


def local(tokens, grad_out, lang_ids, gate_weight, up_weight, down_weight):
    vmem = pl.BlockSpec(memory_space=pltpu.VMEM)
    anyspace = pl.BlockSpec(memory_space=pl.ANY)
    hbm = pl.BlockSpec(memory_space=pltpu.HBM)
    dma = pltpu.SemaphoreType.DMA
    scratch = [
        pltpu.VMEM((CHUNK, 128), BF16),
        pltpu.VMEM((CHUNK, 128), BF16),
        pltpu.VMEM((1, 128), jnp.int32),
        pltpu.VMEM((D, HID), BF16),
        pltpu.VMEM((D, HID), BF16),
        pltpu.VMEM((HID, D), BF16),
        pltpu.VMEM((D, HID), BF16),
        pltpu.VMEM((N, CHUNK, 128), BF16),
        pltpu.VMEM((N, CHUNK, 128), BF16),
        pltpu.VMEM((64, CHUNK, XD), BF16),
        pltpu.VMEM((N * 128, XD), BF16),
        pltpu.VMEM((N * 64, 128), BF16),
        pltpu.VMEM((2 * HID, MAIN), F32),
        pltpu.VMEM((HID, MAIN), F32),
        pltpu.VMEM((3 * HID, 128), F32),
        pltpu.VMEM((2 * HID, DR + 128), BF16),
        pltpu.VMEM((HID, DR), BF16),
        pltpu.VMEM((64, CHUNK, DR), F32),
        pltpu.VMEM((2, 2, 2, 4, CHUNK, XD), BF16),
        pltpu.VMEM((2, 2, 2, 4, CHUNK, XD), BF16),
        pltpu.VMEM((N, CHUNK, DR), BF16),
        pltpu.VMEM((N, CHUNK, DR), BF16),
        pltpu.VMEM((N, CHUNK, 128), BF16),
        pltpu.VMEM((N, CHUNK, 128), BF16),
        pltpu.VMEM((D, HID), BF16),
        pltpu.VMEM((D, HID), BF16),
        pltpu.VMEM((HID, D), BF16),
        dma((3,)),
        dma((3,)),
        dma((N,)), dma((N,)),
        dma((N,)), dma((N,)),
        dma((2, 2, 4, 4)), dma((2, 2, 4, 4)),
        dma((2, 2, 2, 4)), dma((2, 2, 2, 4)),
        dma((N,)), dma((N,)),
        dma((N,)), dma((N,)),
        dma((3, N)),
    ]
    shapes = (
        jax.ShapeDtypeStruct((CHUNK, 128), BF16),
        jax.ShapeDtypeStruct((D, HID), BF16),
        jax.ShapeDtypeStruct((D, HID), BF16),
        jax.ShapeDtypeStruct((HID, D), BF16),
    )
    out = pl.pallas_call(
        kernel,
        out_shape=shapes,
        in_specs=[hbm] * 6,
        out_specs=(vmem, anyspace, anyspace, anyspace),
        scratch_shapes=scratch,
        compiler_params=pltpu.CompilerParams(
            collective_id=0, has_side_effects=True, vmem_limit_bytes=103 * 512 * 1024
        ),
        cost_estimate=pl.CostEstimate(
            flops=16 * 320 * D * HID, bytes_accessed=6 * D * HID * 2, transcendentals=320 * HID
        ),
    )(
        tokens.T, grad_out.T, lang_ids.T, gate_weight[0], up_weight[0], down_weight[0]
    )
    out = pl.pallas_call(
        copy_kernel,
        out_shape=shapes,
        in_specs=[vmem, anyspace, anyspace, anyspace],
        out_specs=(vmem, hbm, hbm, hbm),
        scratch_shapes=[dma((3,))],
        compiler_params=pltpu.CompilerParams(vmem_limit_bytes=8 * 1024 * 1024),
    )(*out)
    return out[0].T, out[1][None], out[2][None], out[3][None]


def solution(mesh):
    in_specs = (
        P("expert", "hidden"),
        P("expert", "hidden"),
        P("expert", None),
        P("expert", None, "hidden"),
        P("expert", None, "hidden"),
        P("expert", "hidden", None),
    )
    out_specs = (
        P("expert", "hidden"),
        P("expert", None, "hidden"),
        P("expert", None, "hidden"),
        P("expert", "hidden", None),
    )
    return jax.shard_map(local, mesh=mesh, in_specs=in_specs, out_specs=out_specs, check_vma=False)
```

```python
import jax
import jax.numpy as jnp
from jax import lax
from jax.experimental import pallas as pl
from jax.experimental.pallas import tpu as pltpu
from jax.sharding import PartitionSpec as P

MESH = pl.DeviceIdType.MESH
BF16 = jnp.bfloat16
F32 = jnp.float32

N = 8
CAP = 40
CHUNK = 48
HID = 128
D = 64 * CHUNK
MAIN = 256
XD = 640
PART = 16
DR = 384


def tn(left, right):
    return lax.dot_general(left, right, (((0,), (0,)), ((), ())), preferred_element_type=F32)


def nt(left, right):
    return lax.dot_general(left, right, (((1,), (1,)), ((), ())), preferred_element_type=F32)


def nn(left, right):
    return lax.dot_general(left, right, (((1,), (0,)), ((), ())), preferred_element_type=F32)


def iota(shape, dim):
    return lax.broadcasted_iota(jnp.int32, shape, dim)


def off(i, odd):
    return 2 * i - 4 + odd


MESSAGES = (
    ((4, 1, ()), (2, 1, ()), (3, 2, (0,)), (1, 1, (1, 2))),
    ((3, 1, ()), (2, 1, (0,)), (1, 1, (1,))),
)
PEERS = (4, 3, 5, 2, 6, 1, 7)


def kernel(
    tok_ref, wg_hbm, wu_hbm, wd_hbm,
    gt_ref, gg_hbm, gu_hbm, gd_hbm,
    wg, wu, wd, wdt, msg, blk, xd, place, oht, acc_gu, acc_d, acc_t, gcat, hcat,
    part, rsend, rrecv, ssend, srecv, bsend, brecv, gg, gu, gd,
    wsem, a_s, a_r, m_s, m_r, g_s, g_r, r_s, r_r, s_s, s_r, b_s, b_r, osem,
):
    e = lax.axis_index("expert")
    hid = lax.axis_index("hidden")
    core = lax.rem(e, 2)
    y, z = hid // N, lax.rem(hid, N)
    own = lax.rem(y + z + core, 2)
    way = (own, 1 - own)

    def wrap(v):
        return lax.rem(v + 2 * N, N)

    at = (y + own * (z - y), z + own * (y - z))
    stride = (N - 7 * own, 1 + 7 * own)
    table = [[wrap(at[q] + k) * stride[q] for k in range(N)] for q in (0, 1)]
    sides = [[lax.rem((at[q] + odd) // 2, 2) for odd in (0, 1)] for q in (0, 1)]

    def along(q, d):
        if isinstance(d, int):
            return table[q][d % N]
        return wrap(at[q] + d) * stride[q]

    def hx(q, du, dv):
        return along(q, du) + along(1 - q, dv)

    def side(q, odd):
        return sides[q][odd]

    def either(sel, values):
        return values[0] + sel * (values[1] - values[0])

    def chunk_of(q, sel, i, odd, dv):
        if isinstance(sel, int):
            return hx(q, off(i + sel, odd), dv)
        return either(sel, [along(q, off(i + k, odd)) for k in (0, 1)]) + along(1 - q, dv)

    def rows(h):
        return pl.ds(pl.multiple_of(h * CHUNK, CHUNK), CHUNK)

    def remote(src, dst, ss, rs, dev):
        return pltpu.make_async_remote_copy(
            src_ref=src, dst_ref=dst, send_sem=ss, recv_sem=rs, device_id=dev, device_id_type=MESH
        )

    bar = pltpu.get_barrier_semaphore()
    for j in PEERS:
        pl.semaphore_signal(bar, inc=1, device_id={"hidden": hx(0, j, 0)}, device_id_type=MESH)
        if j != 4:
            pl.semaphore_signal(bar, inc=1, device_id={"hidden": hx(1, j, 0)}, device_id_type=MESH)
    for j in PEERS:
        pl.semaphore_signal(bar, inc=1, device_id={"expert": wrap(e + j)}, device_id_type=MESH)

    loads = [
        pltpu.make_async_copy(src, dst, wsem.at[k])
        for k, (src, dst) in enumerate(((wg_hbm, wg), (wu_hbm, wu), (wd_hbm, wd)))
    ]
    for c in loads:
        c.start()

    lang = tok_ref[2 * CHUNK : 2 * CHUNK + 1, :].astype(jnp.int32)
    member = iota((N, 128), 0) == lang
    earlier = (iota((128, 128), 0) < iota((128, 128), 1)).astype(BF16)
    before = nn(member.astype(BF16), earlier)
    slot = jnp.sum(jnp.where(member, before, 0.0), axis=0, keepdims=True).astype(jnp.int32)
    oht[...] = (iota((N * 64, 128), 0) == lang * 64 + slot).astype(BF16)
    out = nt(tok_ref[0 : 2 * CHUNK, :].astype(BF16), oht[...])
    low = iota((CHUNK, 128), 1) < 64
    for k in range(N):
        tile = slice(k // 2 * 128, k // 2 * 128 + 128)
        x_k, dy_k = out[0:CHUNK, tile], out[CHUNK : 2 * CHUNK, tile]
        if k % 2 == 0:
            dy_k = pltpu.roll(dy_k, 64, 1)
        else:
            x_k = pltpu.roll(x_k, 64, 1)
        msg[k] = jnp.where(low, x_k, dy_k).astype(BF16)

    pl.semaphore_wait(bar, 2 * (N - 1) + 6)

    def to_expert(j, src, dst, ss, rs):
        return remote(src.at[wrap(e + j)], dst.at[e], ss.at[j], rs.at[j], {"expert": wrap(e + j)})

    a2a = [to_expert(j, msg, blk, a_s, a_r) for j in PEERS]
    for c in a2a:
        c.start()
    blk[e] = msg[e]

    r1 = iota((N * 128, 1), 0)
    blk_i, j_i = r1 // 128, lax.rem(r1, 128)
    is_dy = j_i >= 64
    jj = jnp.where(is_dy, j_i - 64, j_i)
    pos = blk_i * CAP + jj
    lane = jnp.where(pos < MAIN, pos + jnp.where(is_dy, MAIN, 0), pos + jnp.where(is_dy, MAIN + 64, MAIN))
    lane = jnp.where(jj < CAP, lane, -1)
    place[...] = (iota((N * 128, XD), 1) == lane).astype(BF16)

    for c in loads:
        c.wait()
    for k in range(D // 128):
        wdt[pl.ds(k * 128, 128), :] = wd[:, k * 128 : (k + 1) * 128].T
    acc_gu[...] = jnp.zeros_like(acc_gu)
    acc_d[...] = jnp.zeros_like(acc_d)
    acc_t[...] = jnp.zeros_like(acc_t)

    for c in a2a:
        c.wait()
    cat = jnp.concatenate([blk[k] for k in range(N)], axis=1)
    xd[hid] = nn(cat, place[...]).astype(BF16)

    def small(k, q, chunk, to):
        h = hx(q, chunk, 0)
        return remote(xd.at[h], xd.at[h], m_s.at[k], m_r.at[k], {"hidden": hx(q, to, 0)})

    def small_recv(k):
        h = hx(k % 2, k, 0)
        remote(xd.at[h], xd.at[h], m_s.at[k], m_r.at[k], {"hidden": hid}).wait_recv()

    def big(q, i, d, s, sel=0):
        to = 1 - 2 * d
        h = chunk_of(q, sel, i, (s + q) % 2, -to * s)
        c, i = way[q], i + sel
        return remote(
            xd.at[h], xd.at[h], g_s.at[c, d, s, i], g_r.at[c, d, s, i], {"hidden": hx(q, 0, to)}
        )

    def big_recv(q, i, d, s, sel=0):
        to = 1 - 2 * d
        h = chunk_of(q, sel, i, (s + 1 + q) % 2, -to * (s + 1))
        c, i = way[q], i + sel
        remote(xd.at[h], xd.at[h], g_s.at[c, d, s, i], g_r.at[c, d, s, i], {"hidden": hid}).wait_recv()

    def goes_far(q, d, s):
        c = side(q, (s + q) % 2)
        return c if d == 0 else 1 - c

    def stays(q, d, s):
        return 1 - goes_far(q, d, s)

    def send_big(q, i, s):
        for d in (0, 1):
            if s > 0:
                big_recv(q, i, d, s - 1)
            big(q, i, d, s).start()

    turn = side(0, 0)
    far = 2 - 4 * turn
    sends = [small(1, 0, 0, -1), small(7, 0, 0, 1), small(2, 0, 0, -2), small(6, 0, 0, 2)]
    relay = [small(3, 0, 2, -1), small(5, 0, -2, 1), small(4, 0, far, -far)]
    sends[0].start()
    sends[1].start()
    send_big(0, 2, 0)
    sends[2].start()
    sends[3].start()
    small_recv(1)
    send_big(1, 2, 0)
    small_recv(7)
    send_big(1, 1, 0)
    small_recv(2)
    relay[0].start()
    small_recv(6)
    relay[1].start()
    relay[2].start()
    send_big(0, 3, 0)
    send_big(0, 1, 0)
    small_recv(3)
    send_big(1, 3, 0)
    small_recv(5)
    send_big(1, 0, 0)
    small_recv(4)
    send_big(0, 0, 0)

    def forward(hs):
        left = jnp.concatenate(
            [jnp.concatenate([wg[rows(h), :], wu[rows(h), :], wdt[rows(h), :]], axis=1) for h in hs], axis=0
        )
        right = jnp.concatenate([xd[h] for h in hs], axis=0)
        acc_gu[...] += tn(left[:, 0 : 2 * HID], right[:, 0:MAIN])
        acc_d[...] += tn(left[:, 2 * HID : 3 * HID], right[:, MAIN : 2 * MAIN])
        acc_t[...] += tn(left, right[:, 2 * MAIN : XD])

    def column(dist):
        return [hx(q, off(i, (q + dist) % 2), dist) for q in (0, 1) for i in range(4)]

    forward(column(0))
    for s in range(1, 4):
        if s < 3:
            for pick in (goes_far, stays):
                for j in (1, 0):
                    for q in (0, 1):
                        for d in (0, 1):
                            sel = pick(q, d, s)
                            big_recv(q, 2 * j, d, s - 1, sel)
                            big(q, 2 * j, d, s, sel).start()
        else:
            for j in (0, 1):
                for q in (0, 1):
                    for d in (0, 1):
                        sel = goes_far(q, d, 3)
                        big_recv(q, 2 * j, d, 2, sel)
                        big(q, 2 * j, d, 3, sel).start()
            for q in (0, 1):
                for d in (0, 1):
                    for j in (0, 1):
                        big_recv(q, 2 * j, d, 2, stays(q, d, 3))

        def two(k, carry):
            forward(column((1 - 2 * k) * s))
            return carry

        lax.fori_loop(0, 2, two, 0)

    for q in (0, 1):
        for d in (0, 1):
            for j in (0, 1):
                big_recv(q, 2 * j, d, 3, goes_far(q, d, 4))
    forward(column(4))

    def units(gate, up, dh):
        sig = jax.nn.sigmoid(gate)
        act = gate * sig
        return (
            (act * up).astype(BF16),
            (dh * up * sig * (1.0 + gate * (1.0 - sig))).astype(BF16),
            (dh * act).astype(BF16),
        )

    h_m, g_m, u_m = units(acc_gu[0:HID, :], acc_gu[HID : 2 * HID, :], acc_d[...])
    tail = acc_t[...]
    dh_t = pltpu.roll(tail[2 * HID : 3 * HID, :], 64, 1)
    h_t, g_t, u_t = units(tail[0:HID, :], tail[HID : 2 * HID, :], dh_t)
    low_h = iota((HID, 128), 1) < 64
    for k, (m, t) in enumerate(((g_m, g_t), (u_m, u_t))):
        span = slice(k * HID, (k + 1) * HID)
        t = jnp.where(low_h, t.astype(F32), 0.0)
        gcat[span, 0:MAIN] = m
        gcat[span, MAIN:DR] = t.astype(BF16)
        gcat[span, DR : DR + 128] = pltpu.roll(t, 64, 1).astype(BF16)
    hcat[:, 0:MAIN] = h_m
    hcat[:, MAIN:DR] = pltpu.roll(jnp.where(low_h, h_t.astype(F32), 0.0), 64, 1).astype(BF16)

    def partial_sums(dist):
        hs = column(dist)
        left = jnp.concatenate(
            [jnp.concatenate([wg[rows(h), :], wu[rows(h), :]], axis=1) for h in hs], axis=0
        )
        res = nn(left, gcat[...])
        for n, h in enumerate(hs):
            block = res[n * CHUNK : (n + 1) * CHUNK]
            part[h, :, 0:MAIN] = block[:, 0:MAIN]
            part[h, :, MAIN:DR] = block[:, MAIN:DR] if n % 4 < 2 else block[:, DR : DR + 128]

    def reduce_copy(q, d, short, m, n):
        place = (way[q], d, short, m, n)
        hops = MESSAGES[short][m][1] if isinstance(m, int) else 1
        to = hops * (1 - 2 * d)
        return remote(
            rsend.at[place], rrecv.at[place], r_s.at[place], r_r.at[place], {"hidden": hx(q, 0, to)}
        )

    def pair_parts(q, sel, odd, dist, span):
        h0, h1 = [chunk_of(q, sel, i, odd, dist) for i in (0, 2)]
        return [part[h0, span, 0:MAIN], part[h1, span, 0:MAIN], part[h0, span, MAIN:DR] + part[h1, span, MAIN:DR]]

    def add_message(values, message):
        spans = ((0, MAIN), (MAIN, 2 * MAIN), (2 * MAIN, XD))
        return [v + message[:, lo:hi].astype(F32) for v, (lo, hi) in zip(values, spans)]

    def reduce_step(q, d, short, m, n):
        dist, _, merged = MESSAGES[short][m]
        odd = (q + dist) % 2
        sel = side(q, odd)
        sel = sel if d == short else 1 - sel
        values = pair_parts(q, sel, odd, (1 - 2 * d) * dist, slice(n * PART, (n + 1) * PART))
        c = way[q]
        for k in merged:
            reduce_copy(q, d, short, k, n).wait_recv()
            values = add_message(values, rrecv[c, d, short, k, n])
        rsend[c, d, short, m, n] = jnp.concatenate([v.astype(BF16) for v in values], axis=1)
        reduce_copy(q, d, short, m, n).start()

    def reduce_send(short, m):
        for n in range(CHUNK // PART):
            for q in (0, 1):
                for d in (0, 1):
                    reduce_step(q, d, short, m, n)

    def weight_grads(g):
        span = pl.ds(pl.multiple_of(g * N * CHUNK, N * CHUNK), N * CHUNK)
        feat = xd[pl.ds(g * N, N)].reshape(N * CHUNK, XD)
        x_rows = jnp.concatenate([feat[:, 0:MAIN], feat[:, 2 * MAIN : XD]], axis=1)
        dy_rows = feat[:, MAIN:XD]
        pair = nt(x_rows, gcat[:, 0:DR]).astype(BF16)
        gg[span, :] = pair[:, 0:HID]
        gu[span, :] = pair[:, HID : 2 * HID]
        gd[:, span] = nt(hcat[...], dy_rows).astype(BF16)
        for k, (src, dst) in enumerate(((gg, gg_hbm), (gu, gu_hbm))):
            pltpu.make_async_copy(src.at[span, :], dst.at[span, :], osem.at[k, g]).start()
        pltpu.make_async_copy(gd.at[:, span], gd_hbm.at[:, span], osem.at[2, g]).start()

    def grads(lo, hi):
        def one(g, carry):
            weight_grads(g)
            return carry

        lax.fori_loop(lo, hi, one, 0)

    partial_sums(4)
    reduce_send(0, 0)

    def near(dist):
        def both(k, carry):
            partial_sums((1 - 2 * k) * dist)
            return carry

        lax.fori_loop(0, 2, both, 0)

    near(3)
    reduce_send(1, 0)
    near(2)
    reduce_send(0, 1)
    near(1)
    partial_sums(0)
    reduce_send(0, 2)
    reduce_send(1, 1)
    grads(0, 4)
    reduce_send(0, 3)
    reduce_send(1, 2)
    grads(4, 8)

    def small_sum(k, q):
        return remote(ssend.at[k], srecv.at[k], s_s.at[k], s_r.at[k], {"hidden": hx(q, k, 0)})

    for q, sel in ((0, 0), (1, 0), (1, 1), (0, 1)):
        bit = lax.rem(side(q, q) + sel, 2)
        c = way[q]
        values = pair_parts(q, sel, q, 0, slice(0, CHUNK))
        for d, short in ((0, bit), (1, 1 - bit)):
            last = 3 - short
            for n in range(CHUNK // PART):
                reduce_copy(q, d, short, last, n).wait_recv()
            values = add_message(values, rrecv[c, d, short, last].reshape(CHUNK, XD))
        for j in (0, 1):
            k = off(sel + 2 * j, q) % N
            if k == 0:
                main, high = values[1], values[2]
            else:
                ssend[k] = jnp.concatenate([values[j].astype(BF16), values[2].astype(BF16)], axis=1)
                small_sum(k, q).start()
    low_sum = jnp.zeros((CHUNK, 128), F32)

    p_i = iota((DR, N * 128), 0)
    c_i = iota((DR, N * 128), 1)
    j_c = lax.rem(c_i, 128) - 64 * core
    pick = ((p_i == (c_i // 128) * CAP + j_c) & (j_c >= 0) & (j_c < CAP)).astype(BF16)

    for k in (1, 7, 2, 6, 3, 5, 4):
        remote(ssend.at[k], srecv.at[k], s_s.at[k], s_r.at[k], {"hidden": hid}).wait_recv()
        main = main + srecv[k, :, 0:MAIN].astype(F32)
        if k >= 4:
            low_sum = low_sum + srecv[k, :, MAIN:DR].astype(F32)
        else:
            high = high + srecv[k, :, MAIN:DR].astype(F32)
    tail = low_sum + pltpu.roll(high, 64, 1)
    total = jnp.concatenate([main.astype(BF16), tail.astype(BF16)], axis=1)
    back = nn(total, pick).astype(BF16)
    for k in range(N):
        bsend[k] = back[:, k * 128 : (k + 1) * 128]
    home = [to_expert(j, bsend, brecv, b_s, b_r) for j in PEERS]
    for c in home:
        c.start()
    brecv[e] = bsend[e]

    for c in sends + relay:
        c.wait_send()
    for q in (0, 1):
        for d in (0, 1):
            for s in range(3):
                for i in range(4):
                    big(q, i, d, s).wait_send()
            for j in (0, 1):
                big(q, 2 * j, d, 3, goes_far(q, d, 3)).wait_send()
            for short in (0, 1):
                for s in range(4 - short):
                    for n in range(CHUNK // PART):
                        reduce_copy(q, d, short, s, n).wait_send()
    for k in range(1, N):
        small_sum(k, k % 2).wait_send()

    def flush(g, carry):
        span = pl.ds(pl.multiple_of(g * N * CHUNK, N * CHUNK), N * CHUNK)
        for k, (src, dst) in enumerate(((gg, gg_hbm), (gu, gu_hbm))):
            pltpu.make_async_copy(src.at[span, :], dst.at[span, :], osem.at[k, g]).wait()
        pltpu.make_async_copy(gd.at[:, span], gd_hbm.at[:, span], osem.at[2, g]).wait()
        return carry

    lax.fori_loop(0, N, flush, 0)

    for c in home:
        c.wait()
    cat = jnp.concatenate([jnp.where(low, brecv[k], brecv[k + 1]) for k in range(0, N, 2)], axis=1)
    gt_ref[...] = nn(cat, oht[...]).astype(BF16)


def copy_kernel(gt, gg, gu, gd, gt_out, gg_out, gu_out, gd_out, sem):
    copies = [
        pltpu.make_async_copy(src, dst, sem.at[k])
        for k, (src, dst) in enumerate(((gg, gg_out), (gu, gu_out), (gd, gd_out)))
    ]
    for c in copies:
        c.start()
    gt_out[...] = gt[...]
    for c in copies:
        c.wait()


def local(tokens, grad_out, lang_ids, gate_weight, up_weight, down_weight):
    vmem = pl.BlockSpec(memory_space=pltpu.VMEM)
    anyspace = pl.BlockSpec(memory_space=pl.ANY)
    hbm = pl.BlockSpec(memory_space=pltpu.HBM)
    dma = pltpu.SemaphoreType.DMA
    scratch = [
        pltpu.VMEM((D, HID), BF16),
        pltpu.VMEM((D, HID), BF16),
        pltpu.VMEM((HID, D), BF16),
        pltpu.VMEM((D, HID), BF16),
        pltpu.VMEM((N, CHUNK, 128), BF16),
        pltpu.VMEM((N, CHUNK, 128), BF16),
        pltpu.VMEM((64, CHUNK, XD), BF16),
        pltpu.VMEM((N * 128, XD), BF16),
        pltpu.VMEM((N * 64, 128), BF16),
        pltpu.VMEM((2 * HID, MAIN), F32),
        pltpu.VMEM((HID, MAIN), F32),
        pltpu.VMEM((3 * HID, 128), F32),
        pltpu.VMEM((2 * HID, DR + 128), BF16),
        pltpu.VMEM((HID, DR), BF16),
        pltpu.VMEM((64, CHUNK, DR), F32),
        pltpu.VMEM((2, 2, 2, 4, CHUNK // PART, PART, XD), BF16),
        pltpu.VMEM((2, 2, 2, 4, CHUNK // PART, PART, XD), BF16),
        pltpu.VMEM((N, CHUNK, DR), BF16),
        pltpu.VMEM((N, CHUNK, DR), BF16),
        pltpu.VMEM((N, CHUNK, 128), BF16),
        pltpu.VMEM((N, CHUNK, 128), BF16),
        pltpu.VMEM((D, HID), BF16),
        pltpu.VMEM((D, HID), BF16),
        pltpu.VMEM((HID, D), BF16),
        dma((3,)),
        dma((N,)), dma((N,)),
        dma((N,)), dma((N,)),
        dma((2, 2, 4, 4)), dma((2, 2, 4, 4)),
        dma((2, 2, 2, 4, CHUNK // PART)), dma((2, 2, 2, 4, CHUNK // PART)),
        dma((N,)), dma((N,)),
        dma((N,)), dma((N,)),
        dma((3, N)),
    ]
    packed = jnp.concatenate([v.T.astype(F32) for v in (tokens, grad_out, lang_ids)], axis=0)
    shapes = (
        jax.ShapeDtypeStruct((CHUNK, 128), BF16),
        jax.ShapeDtypeStruct((D, HID), BF16),
        jax.ShapeDtypeStruct((D, HID), BF16),
        jax.ShapeDtypeStruct((HID, D), BF16),
    )
    out = pl.pallas_call(
        kernel,
        out_shape=shapes,
        in_specs=[vmem] + [hbm] * 3,
        out_specs=(vmem, anyspace, anyspace, anyspace),
        scratch_shapes=scratch,
        compiler_params=pltpu.CompilerParams(
            collective_id=0, has_side_effects=True, vmem_limit_bytes=103 * 512 * 1024
        ),
        cost_estimate=pl.CostEstimate(
            flops=16 * 320 * D * HID, bytes_accessed=6 * D * HID * 2, transcendentals=320 * HID
        ),
    )(
        packed, gate_weight[0], up_weight[0], down_weight[0]
    )
    out = pl.pallas_call(
        copy_kernel,
        out_shape=shapes,
        in_specs=[vmem, anyspace, anyspace, anyspace],
        out_specs=(vmem, hbm, hbm, hbm),
        scratch_shapes=[dma((3,))],
        compiler_params=pltpu.CompilerParams(vmem_limit_bytes=8 * 1024 * 1024),
    )(*out)
    return out[0].T, out[1][None], out[2][None], out[3][None]


def solution(mesh):
    in_specs = (
        P("expert", "hidden"),
        P("expert", "hidden"),
        P("expert", None),
        P("expert", None, "hidden"),
        P("expert", None, "hidden"),
        P("expert", "hidden", None),
    )
    out_specs = (
        P("expert", "hidden"),
        P("expert", None, "hidden"),
        P("expert", None, "hidden"),
        P("expert", "hidden", None),
    )
    return jax.shard_map(local, mesh=mesh, in_specs=in_specs, out_specs=out_specs, check_vma=False)
```

```python
import jax
import jax.numpy as jnp
from jax import lax
from jax.experimental import pallas as pl
from jax.experimental.pallas import tpu as pltpu
from jax.sharding import PartitionSpec as P

MESH = pl.DeviceIdType.MESH
BF16 = jnp.bfloat16
F32 = jnp.float32

N = 8
CAP = 40
CHUNK = 48
HID = 128
D = 64 * CHUNK
MAIN = 256
XD = 640
PART = 48
DR = 384


def tn(left, right):
    return lax.dot_general(left, right, (((0,), (0,)), ((), ())), preferred_element_type=F32)


def nt(left, right):
    return lax.dot_general(left, right, (((1,), (1,)), ((), ())), preferred_element_type=F32)


def nn(left, right):
    return lax.dot_general(left, right, (((1,), (0,)), ((), ())), preferred_element_type=F32)


def iota(shape, dim):
    return lax.broadcasted_iota(jnp.int32, shape, dim)


def off(i, odd):
    return 2 * i - 4 + odd


MESSAGES = (
    ((4, 1, ()), (2, 1, ()), (3, 2, (0,)), (1, 1, (1, 2))),
    ((3, 1, ()), (2, 1, (0,)), (1, 1, (1,))),
)
PEERS = (4, 3, 5, 2, 6, 1, 7)


def kernel(
    tok_ref, lang_ref, wg_hbm, wu_hbm, wd_hbm,
    gt_ref, gg_hbm, gu_hbm, gd_hbm,
    wg, wu, wd, wdt, msg, blk, xd, place, oht, acc_gu, acc_d, acc_t, gcat, hcat,
    part, rsend, rrecv, ssend, srecv, bsend, brecv, gg, gu, gd,
    wsem, a_s, a_r, m_s, m_r, g_s, g_r, r_s, r_r, s_s, s_r, b_s, b_r, osem,
):
    e = lax.axis_index("expert")
    hid = lax.axis_index("hidden")
    core = lax.rem(e, 2)
    y, z = hid // N, lax.rem(hid, N)
    own = lax.rem(y + z + core, 2)
    way = (own, 1 - own)

    def wrap(v):
        return lax.rem(v + 2 * N, N)

    at = (y + own * (z - y), z + own * (y - z))
    stride = (N - 7 * own, 1 + 7 * own)
    table = [[wrap(at[q] + k) * stride[q] for k in range(N)] for q in (0, 1)]
    sides = [[lax.rem((at[q] + odd) // 2, 2) for odd in (0, 1)] for q in (0, 1)]

    def along(q, d):
        if isinstance(d, int):
            return table[q][d % N]
        return wrap(at[q] + d) * stride[q]

    def hx(q, du, dv):
        return along(q, du) + along(1 - q, dv)

    def side(q, odd):
        return sides[q][odd]

    def either(sel, values):
        return values[0] + sel * (values[1] - values[0])

    def chunk_of(q, sel, i, odd, dv):
        if isinstance(sel, int):
            return hx(q, off(i + sel, odd), dv)
        return either(sel, [along(q, off(i + k, odd)) for k in (0, 1)]) + along(1 - q, dv)

    def rows(h):
        return pl.ds(pl.multiple_of(h * CHUNK, CHUNK), CHUNK)

    def remote(src, dst, ss, rs, dev):
        return pltpu.make_async_remote_copy(
            src_ref=src, dst_ref=dst, send_sem=ss, recv_sem=rs, device_id=dev, device_id_type=MESH
        )

    bar = pltpu.get_barrier_semaphore()
    for j in PEERS:
        pl.semaphore_signal(bar, inc=1, device_id={"hidden": hx(0, j, 0)}, device_id_type=MESH)
        if j != 4:
            pl.semaphore_signal(bar, inc=1, device_id={"hidden": hx(1, j, 0)}, device_id_type=MESH)
    for j in PEERS:
        pl.semaphore_signal(bar, inc=1, device_id={"expert": wrap(e + j)}, device_id_type=MESH)

    loads = [
        pltpu.make_async_copy(src, dst, wsem.at[k])
        for k, (src, dst) in enumerate(((wg_hbm, wg), (wu_hbm, wu), (wd_hbm, wd)))
    ]
    for c in loads:
        c.start()

    lang = lang_ref[...]
    member = iota((N, 128), 0) == lang
    earlier = (iota((128, 128), 0) < iota((128, 128), 1)).astype(BF16)
    before = nn(member.astype(BF16), earlier)
    slot = jnp.sum(jnp.where(member, before, 0.0), axis=0, keepdims=True).astype(jnp.int32)
    oht[...] = (iota((N * 64, 128), 0) == lang * 64 + slot).astype(BF16)
    out = nt(tok_ref[...].astype(BF16), oht[...])
    low = iota((CHUNK, 128), 1) < 64
    for k in range(N):
        tile = slice(k // 2 * 128, k // 2 * 128 + 128)
        x_k, dy_k = out[0:CHUNK, tile], out[CHUNK : 2 * CHUNK, tile]
        if k % 2 == 0:
            dy_k = pltpu.roll(dy_k, 64, 1)
        else:
            x_k = pltpu.roll(x_k, 64, 1)
        msg[k] = jnp.where(low, x_k, dy_k).astype(BF16)

    pl.semaphore_wait(bar, 2 * (N - 1) + 6)

    def to_expert(j, src, dst, ss, rs):
        return remote(src.at[wrap(e + j)], dst.at[e], ss.at[j], rs.at[j], {"expert": wrap(e + j)})

    a2a = [to_expert(j, msg, blk, a_s, a_r) for j in PEERS]
    for c in a2a:
        c.start()
    blk[e] = msg[e]

    r1 = iota((N * 128, 1), 0)
    blk_i, j_i = r1 // 128, lax.rem(r1, 128)
    is_dy = j_i >= 64
    jj = jnp.where(is_dy, j_i - 64, j_i)
    pos = blk_i * CAP + jj
    lane = jnp.where(pos < MAIN, pos + jnp.where(is_dy, MAIN, 0), pos + jnp.where(is_dy, MAIN + 64, MAIN))
    lane = jnp.where(jj < CAP, lane, -1)
    place[...] = (iota((N * 128, XD), 1) == lane).astype(BF16)

    for c in a2a:
        c.wait_recv()
    cat = jnp.concatenate([blk[k] for k in range(N)], axis=1)
    xd[hid] = nn(cat, place[...]).astype(BF16)

    def small(k, q, chunk, to):
        h = hx(q, chunk, 0)
        return remote(xd.at[h], xd.at[h], m_s.at[k], m_r.at[k], {"hidden": hx(q, to, 0)})

    def small_recv(k):
        h = hx(k % 2, k, 0)
        remote(xd.at[h], xd.at[h], m_s.at[k], m_r.at[k], {"hidden": hid}).wait_recv()

    def big(q, i, d, s, sel=0):
        to = 1 - 2 * d
        h = chunk_of(q, sel, i, (s + q) % 2, -to * s)
        c, i = way[q], i + sel
        return remote(
            xd.at[h], xd.at[h], g_s.at[c, d, s, i], g_r.at[c, d, s, i], {"hidden": hx(q, 0, to)}
        )

    def big_recv(q, i, d, s, sel=0):
        to = 1 - 2 * d
        h = chunk_of(q, sel, i, (s + 1 + q) % 2, -to * (s + 1))
        c, i = way[q], i + sel
        remote(xd.at[h], xd.at[h], g_s.at[c, d, s, i], g_r.at[c, d, s, i], {"hidden": hid}).wait_recv()

    def goes_far(q, d, s):
        c = side(q, (s + q) % 2)
        return c if d == 0 else 1 - c

    def stays(q, d, s):
        return 1 - goes_far(q, d, s)

    def send_big(q, i, s):
        for d in (0, 1):
            if s > 0:
                big_recv(q, i, d, s - 1)
            big(q, i, d, s).start()

    turn = side(0, 0)
    far = 2 - 4 * turn
    sends = [small(1, 0, 0, -1), small(7, 0, 0, 1), small(2, 0, 0, -2), small(6, 0, 0, 2)]
    relay = [small(3, 0, 2, -1), small(5, 0, -2, 1), small(4, 0, far, -far)]
    sends[0].start()
    sends[1].start()
    send_big(0, 2, 0)
    sends[2].start()
    sends[3].start()
    for c in loads:
        c.wait()
    for k in range(D // 128):
        wdt[pl.ds(k * 128, 128), :] = wd[:, k * 128 : (k + 1) * 128].T
    acc_gu[...] = jnp.zeros_like(acc_gu)
    acc_d[...] = jnp.zeros_like(acc_d)
    acc_t[...] = jnp.zeros_like(acc_t)
    small_recv(1)
    send_big(1, 2, 0)
    small_recv(7)
    send_big(1, 1, 0)
    small_recv(2)
    relay[0].start()
    small_recv(6)
    relay[1].start()
    relay[2].start()
    send_big(0, 3, 0)
    send_big(0, 1, 0)
    small_recv(3)
    send_big(1, 3, 0)
    small_recv(5)
    send_big(1, 0, 0)
    small_recv(4)
    send_big(0, 0, 0)

    def forward(hs):
        left = jnp.concatenate(
            [jnp.concatenate([wg[rows(h), :], wu[rows(h), :], wdt[rows(h), :]], axis=1) for h in hs], axis=0
        )
        right = jnp.concatenate([xd[h] for h in hs], axis=0)
        acc_gu[...] += tn(left[:, 0 : 2 * HID], right[:, 0:MAIN])
        acc_d[...] += tn(left[:, 2 * HID : 3 * HID], right[:, MAIN : 2 * MAIN])
        acc_t[...] += tn(left, right[:, 2 * MAIN : XD])

    def column(dist):
        return [hx(q, off(i, (q + dist) % 2), dist) for q in (0, 1) for i in range(4)]

    forward(column(0))
    for s in range(1, 4):
        if s < 3:
            for pick in (goes_far, stays):
                for j in (1, 0):
                    for q in (0, 1):
                        for d in (0, 1):
                            sel = pick(q, d, s)
                            big_recv(q, 2 * j, d, s - 1, sel)
                            big(q, 2 * j, d, s, sel).start()
        else:
            for j in (0, 1):
                for q in (0, 1):
                    for d in (0, 1):
                        sel = goes_far(q, d, 3)
                        big_recv(q, 2 * j, d, 2, sel)
                        big(q, 2 * j, d, 3, sel).start()
            for q in (0, 1):
                for d in (0, 1):
                    for j in (0, 1):
                        big_recv(q, 2 * j, d, 2, stays(q, d, 3))

        def two(k, carry):
            forward(column((1 - 2 * k) * s))
            return carry

        lax.fori_loop(0, 2, two, 0)

    for q in (0, 1):
        for d in (0, 1):
            for j in (0, 1):
                big_recv(q, 2 * j, d, 3, goes_far(q, d, 4))
    forward(column(4))

    def units(gate, up, dh):
        sig = jax.nn.sigmoid(gate)
        act = gate * sig
        return (
            (act * up).astype(BF16),
            (dh * up * sig * (1.0 + gate * (1.0 - sig))).astype(BF16),
            (dh * act).astype(BF16),
        )

    h_m, g_m, u_m = units(acc_gu[0:HID, :], acc_gu[HID : 2 * HID, :], acc_d[...])
    tail = acc_t[...]
    dh_t = pltpu.roll(tail[2 * HID : 3 * HID, :], 64, 1)
    h_t, g_t, u_t = units(tail[0:HID, :], tail[HID : 2 * HID, :], dh_t)
    low_h = iota((HID, 128), 1) < 64
    for k, (m, t) in enumerate(((g_m, g_t), (u_m, u_t))):
        span = slice(k * HID, (k + 1) * HID)
        t = jnp.where(low_h, t.astype(F32), 0.0)
        gcat[span, 0:MAIN] = m
        gcat[span, MAIN:DR] = t.astype(BF16)
        gcat[span, DR : DR + 128] = pltpu.roll(t, 64, 1).astype(BF16)
    hcat[:, 0:MAIN] = h_m
    hcat[:, MAIN:DR] = pltpu.roll(jnp.where(low_h, h_t.astype(F32), 0.0), 64, 1).astype(BF16)

    def partial_sums(dist):
        hs = column(dist)
        left = jnp.concatenate(
            [jnp.concatenate([wg[rows(h), :], wu[rows(h), :]], axis=1) for h in hs], axis=0
        )
        res = nn(left, gcat[...])
        for n, h in enumerate(hs):
            block = res[n * CHUNK : (n + 1) * CHUNK]
            part[h, :, 0:MAIN] = block[:, 0:MAIN]
            part[h, :, MAIN:DR] = block[:, MAIN:DR] if n % 4 < 2 else block[:, DR : DR + 128]

    def reduce_copy(q, d, short, m, n):
        place = (way[q], d, short, m, n)
        hops = MESSAGES[short][m][1] if isinstance(m, int) else 1
        to = hops * (1 - 2 * d)
        return remote(
            rsend.at[place], rrecv.at[place], r_s.at[place], r_r.at[place], {"hidden": hx(q, 0, to)}
        )

    def pair_parts(q, sel, odd, dist, span):
        h0, h1 = [chunk_of(q, sel, i, odd, dist) for i in (0, 2)]
        return [part[h0, span, 0:MAIN], part[h1, span, 0:MAIN], part[h0, span, MAIN:DR] + part[h1, span, MAIN:DR]]

    def add_message(values, message):
        spans = ((0, MAIN), (MAIN, 2 * MAIN), (2 * MAIN, XD))
        return [v + message[:, lo:hi].astype(F32) for v, (lo, hi) in zip(values, spans)]

    def reduce_step(q, d, short, m, n):
        dist, _, merged = MESSAGES[short][m]
        odd = (q + dist) % 2
        sel = side(q, odd)
        sel = sel if d == short else 1 - sel
        values = pair_parts(q, sel, odd, (1 - 2 * d) * dist, slice(n * PART, (n + 1) * PART))
        c = way[q]
        for k in merged:
            reduce_copy(q, d, short, k, n).wait_recv()
            values = add_message(values, rrecv[c, d, short, k, n])
        rsend[c, d, short, m, n] = jnp.concatenate([v.astype(BF16) for v in values], axis=1)
        reduce_copy(q, d, short, m, n).start()

    def reduce_send(short, m):
        for n in range(CHUNK // PART):
            for q in (0, 1):
                for d in (0, 1):
                    reduce_step(q, d, short, m, n)

    def weight_grads(g):
        span = pl.ds(pl.multiple_of(g * N * CHUNK, N * CHUNK), N * CHUNK)
        feat = xd[pl.ds(g * N, N)].reshape(N * CHUNK, XD)
        x_rows = jnp.concatenate([feat[:, 0:MAIN], feat[:, 2 * MAIN : XD]], axis=1)
        dy_rows = feat[:, MAIN:XD]
        pair = nt(x_rows, gcat[:, 0:DR]).astype(BF16)
        gg[span, :] = pair[:, 0:HID]
        gu[span, :] = pair[:, HID : 2 * HID]
        gd[:, span] = nt(hcat[...], dy_rows).astype(BF16)
        for k, (src, dst) in enumerate(((gg, gg_hbm), (gu, gu_hbm))):
            pltpu.make_async_copy(src.at[span, :], dst.at[span, :], osem.at[k, g]).start()
        pltpu.make_async_copy(gd.at[:, span], gd_hbm.at[:, span], osem.at[2, g]).start()

    def grads(lo, hi):
        def one(g, carry):
            weight_grads(g)
            return carry

        lax.fori_loop(lo, hi, one, 0)

    partial_sums(4)
    reduce_send(0, 0)

    def near(dist):
        def both(k, carry):
            partial_sums((1 - 2 * k) * dist)
            return carry

        lax.fori_loop(0, 2, both, 0)

    near(3)
    reduce_send(1, 0)
    near(2)
    reduce_send(0, 1)
    near(1)
    partial_sums(0)
    reduce_send(0, 2)
    reduce_send(1, 1)
    grads(0, 4)
    reduce_send(0, 3)
    reduce_send(1, 2)
    grads(4, 8)

    def small_sum(k, q):
        return remote(ssend.at[k], srecv.at[k], s_s.at[k], s_r.at[k], {"hidden": hx(q, k, 0)})

    for q, sel in ((0, 0), (1, 0), (1, 1), (0, 1)):
        bit = lax.rem(side(q, q) + sel, 2)
        c = way[q]
        values = pair_parts(q, sel, q, 0, slice(0, CHUNK))
        for d, short in ((0, bit), (1, 1 - bit)):
            last = 3 - short
            for n in range(CHUNK // PART):
                reduce_copy(q, d, short, last, n).wait_recv()
            values = add_message(values, rrecv[c, d, short, last].reshape(CHUNK, XD))
        for j in (0, 1):
            k = off(sel + 2 * j, q) % N
            if k == 0:
                main, high = values[1], values[2]
            else:
                ssend[k] = jnp.concatenate([values[j].astype(BF16), values[2].astype(BF16)], axis=1)
                small_sum(k, q).start()
    for c in a2a:
        c.wait_send()
    for c in sends + relay:
        c.wait_send()
    for q in (0, 1):
        for d in (0, 1):
            for s in range(3):
                for i in range(4):
                    big(q, i, d, s).wait_send()
            for j in (0, 1):
                big(q, 2 * j, d, 3, goes_far(q, d, 3)).wait_send()
            for short in (0, 1):
                for s in range(4 - short):
                    for n in range(CHUNK // PART):
                        reduce_copy(q, d, short, s, n).wait_send()
    low_sum = jnp.zeros((CHUNK, 128), F32)

    p_i = iota((DR, N * 128), 0)
    c_i = iota((DR, N * 128), 1)
    j_c = lax.rem(c_i, 128) - 64 * core
    pick = ((p_i == (c_i // 128) * CAP + j_c) & (j_c >= 0) & (j_c < CAP)).astype(BF16)

    for k in (1, 7, 2, 6, 3, 5, 4):
        remote(ssend.at[k], srecv.at[k], s_s.at[k], s_r.at[k], {"hidden": hid}).wait_recv()
        main = main + srecv[k, :, 0:MAIN].astype(F32)
        if k >= 4:
            low_sum = low_sum + srecv[k, :, MAIN:DR].astype(F32)
        else:
            high = high + srecv[k, :, MAIN:DR].astype(F32)
    tail = low_sum + pltpu.roll(high, 64, 1)
    total = jnp.concatenate([main.astype(BF16), tail.astype(BF16)], axis=1)
    back = nn(total, pick).astype(BF16)
    for k in range(N):
        bsend[k] = back[:, k * 128 : (k + 1) * 128]
    home = [to_expert(j, bsend, brecv, b_s, b_r) for j in PEERS]
    for c in home:
        c.start()
    brecv[e] = bsend[e]

    for k in range(1, N):
        small_sum(k, k % 2).wait_send()
    def flush(g, carry):
        span = pl.ds(pl.multiple_of(g * N * CHUNK, N * CHUNK), N * CHUNK)
        for k, (src, dst) in enumerate(((gg, gg_hbm), (gu, gu_hbm))):
            pltpu.make_async_copy(src.at[span, :], dst.at[span, :], osem.at[k, g]).wait()
        pltpu.make_async_copy(gd.at[:, span], gd_hbm.at[:, span], osem.at[2, g]).wait()
        return carry

    lax.fori_loop(0, N, flush, 0)
    for c in home:
        c.wait()
    cat = jnp.concatenate([jnp.where(low, brecv[k], brecv[k + 1]) for k in range(0, N, 2)], axis=1)
    gt_ref[...] = nn(cat, oht[...]).astype(BF16)


def copy_kernel(gt, gg, gu, gd, gt_out, gg_out, gu_out, gd_out, sem):
    copies = [
        pltpu.make_async_copy(src, dst, sem.at[k])
        for k, (src, dst) in enumerate(((gg, gg_out), (gu, gu_out), (gd, gd_out)))
    ]
    for c in copies:
        c.start()
    gt_out[...] = gt[...]
    for c in copies:
        c.wait()


def local(tokens, grad_out, lang_ids, gate_weight, up_weight, down_weight):
    vmem = pl.BlockSpec(memory_space=pltpu.VMEM)
    anyspace = pl.BlockSpec(memory_space=pl.ANY)
    hbm = pl.BlockSpec(memory_space=pltpu.HBM)
    dma = pltpu.SemaphoreType.DMA
    scratch = [
        pltpu.VMEM((D, HID), BF16),
        pltpu.VMEM((D, HID), BF16),
        pltpu.VMEM((HID, D), BF16),
        pltpu.VMEM((D, HID), BF16),
        pltpu.VMEM((N, CHUNK, 128), BF16),
        pltpu.VMEM((N, CHUNK, 128), BF16),
        pltpu.VMEM((64, CHUNK, XD), BF16),
        pltpu.VMEM((N * 128, XD), BF16),
        pltpu.VMEM((N * 64, 128), BF16),
        pltpu.VMEM((2 * HID, MAIN), F32),
        pltpu.VMEM((HID, MAIN), F32),
        pltpu.VMEM((3 * HID, 128), F32),
        pltpu.VMEM((2 * HID, DR + 128), BF16),
        pltpu.VMEM((HID, DR), BF16),
        pltpu.VMEM((64, CHUNK, DR), F32),
        pltpu.VMEM((2, 2, 2, 4, CHUNK // PART, PART, XD), BF16),
        pltpu.VMEM((2, 2, 2, 4, CHUNK // PART, PART, XD), BF16),
        pltpu.VMEM((N, CHUNK, DR), BF16),
        pltpu.VMEM((N, CHUNK, DR), BF16),
        pltpu.VMEM((N, CHUNK, 128), BF16),
        pltpu.VMEM((N, CHUNK, 128), BF16),
        pltpu.VMEM((D, HID), BF16),
        pltpu.VMEM((D, HID), BF16),
        pltpu.VMEM((HID, D), BF16),
        dma((3,)),
        dma((N,)), dma((N,)),
        dma((N,)), dma((N,)),
        dma((2, 2, 4, 4)), dma((2, 2, 4, 4)),
        dma((2, 2, 2, 4, CHUNK // PART)), dma((2, 2, 2, 4, CHUNK // PART)),
        dma((N,)), dma((N,)),
        dma((N,)), dma((N,)),
        dma((3, N)),
    ]
    packed = jnp.concatenate([v.T.astype(F32) for v in (tokens, grad_out)], axis=0)
    shapes = (
        jax.ShapeDtypeStruct((CHUNK, 128), BF16),
        jax.ShapeDtypeStruct((D, HID), BF16),
        jax.ShapeDtypeStruct((D, HID), BF16),
        jax.ShapeDtypeStruct((HID, D), BF16),
    )
    out = pl.pallas_call(
        kernel,
        out_shape=shapes,
        in_specs=[vmem] * 2 + [hbm] * 3,
        out_specs=(vmem, anyspace, anyspace, anyspace),
        scratch_shapes=scratch,
        compiler_params=pltpu.CompilerParams(
            collective_id=0, has_side_effects=True, vmem_limit_bytes=103 * 512 * 1024
        ),
        cost_estimate=pl.CostEstimate(
            flops=16 * 320 * D * HID, bytes_accessed=6 * D * HID * 2, transcendentals=320 * HID
        ),
    )(
        packed, lang_ids.T, gate_weight[0], up_weight[0], down_weight[0]
    )
    out = pl.pallas_call(
        copy_kernel,
        out_shape=shapes,
        in_specs=[vmem, anyspace, anyspace, anyspace],
        out_specs=(vmem, hbm, hbm, hbm),
        scratch_shapes=[dma((3,))],
        compiler_params=pltpu.CompilerParams(vmem_limit_bytes=8 * 1024 * 1024),
    )(*out)
    return out[0].T, out[1][None], out[2][None], out[3][None]


def solution(mesh):
    in_specs = (
        P("expert", "hidden"),
        P("expert", "hidden"),
        P("expert", None),
        P("expert", None, "hidden"),
        P("expert", None, "hidden"),
        P("expert", "hidden", None),
    )
    out_specs = (
        P("expert", "hidden"),
        P("expert", None, "hidden"),
        P("expert", None, "hidden"),
        P("expert", "hidden", None),
    )
    return jax.shard_map(local, mesh=mesh, in_specs=in_specs, out_specs=out_specs, check_vma=False)
```

```python
import jax
import jax.numpy as jnp
from jax import lax
from jax.experimental import pallas as pl
from jax.experimental.pallas import tpu as pltpu
from jax.sharding import PartitionSpec as P

MESH = pl.DeviceIdType.MESH
BF16 = jnp.bfloat16
F32 = jnp.float32

N = 8
CAP = 40
CHUNK = 48
HID = 128
D = 64 * CHUNK
MAIN = 256
XD = 640
PART = 48
DR = 384


def tn(left, right):
    return lax.dot_general(left, right, (((0,), (0,)), ((), ())), preferred_element_type=F32)


def nt(left, right):
    return lax.dot_general(left, right, (((1,), (1,)), ((), ())), preferred_element_type=F32)


def nn(left, right):
    return lax.dot_general(left, right, (((1,), (0,)), ((), ())), preferred_element_type=F32)


def iota(shape, dim):
    return lax.broadcasted_iota(jnp.int32, shape, dim)


def off(i, odd):
    return 2 * i - 4 + odd


MESSAGES = (
    ((4, 1, ()), (2, 1, ()), (3, 2, (0,)), (1, 1, (1, 2))),
    ((3, 1, ()), (2, 1, (0,)), (1, 1, (1,))),
)
PEERS = (4, 3, 5, 2, 6, 1, 7)


def kernel(
    tok_ref, lang_ref, wg_hbm, wu_hbm, wd_hbm,
    gt_ref, gg_hbm, gu_hbm, gd_hbm,
    wg, wu, wd, wdt, msg, blk, xd, place, oht, acc_gu, acc_d, acc_t, gcat, hcat,
    part, rsend, rrecv, ssend, srecv, bsend, brecv, gg, gu, gd,
    wsem, a_s, a_r, m_s, m_r, g_s, g_r, r_s, r_r, s_s, s_r, b_s, b_r, osem,
):
    e = lax.axis_index("expert")
    hid = lax.axis_index("hidden")
    core = lax.rem(e, 2)
    y, z = hid // N, lax.rem(hid, N)
    own = lax.rem(y + z + core, 2)
    way = (own, 1 - own)

    def wrap(v):
        return lax.rem(v + 2 * N, N)

    at = (y + own * (z - y), z + own * (y - z))
    stride = (N - 7 * own, 1 + 7 * own)
    table = [[wrap(at[q] + k) * stride[q] for k in range(N)] for q in (0, 1)]
    sides = [[lax.rem((at[q] + odd) // 2, 2) for odd in (0, 1)] for q in (0, 1)]

    def along(q, d):
        if isinstance(d, int):
            return table[q][d % N]
        return wrap(at[q] + d) * stride[q]

    def hx(q, du, dv):
        return along(q, du) + along(1 - q, dv)

    def side(q, odd):
        return sides[q][odd]

    def either(sel, values):
        return values[0] + sel * (values[1] - values[0])

    def chunk_of(q, sel, i, odd, dv):
        if isinstance(sel, int):
            return hx(q, off(i + sel, odd), dv)
        return either(sel, [along(q, off(i + k, odd)) for k in (0, 1)]) + along(1 - q, dv)

    def rows(h):
        return pl.ds(pl.multiple_of(h * CHUNK, CHUNK), CHUNK)

    def remote(src, dst, ss, rs, dev):
        return pltpu.make_async_remote_copy(
            src_ref=src, dst_ref=dst, send_sem=ss, recv_sem=rs, device_id=dev, device_id_type=MESH
        )

    bar = pltpu.get_barrier_semaphore()
    for j in PEERS:
        pl.semaphore_signal(bar, inc=1, device_id={"hidden": hx(0, j, 0)}, device_id_type=MESH)
        if j != 4:
            pl.semaphore_signal(bar, inc=1, device_id={"hidden": hx(1, j, 0)}, device_id_type=MESH)
    for j in PEERS:
        pl.semaphore_signal(bar, inc=1, device_id={"expert": wrap(e + j)}, device_id_type=MESH)

    loads = [
        pltpu.make_async_copy(src, dst, wsem.at[k])
        for k, (src, dst) in enumerate(((wg_hbm, wg), (wu_hbm, wu), (wd_hbm, wd)))
    ]
    for c in loads:
        c.start()

    lang = lang_ref[...]
    member = iota((N, 128), 0) == lang
    earlier = (iota((128, 128), 0) < iota((128, 128), 1)).astype(BF16)
    before = nn(member.astype(BF16), earlier)
    slot = jnp.sum(jnp.where(member, before, 0.0), axis=0, keepdims=True).astype(jnp.int32)
    oht[...] = (iota((N * 64, 128), 0) == lang * 64 + slot).astype(BF16)
    out = nt(tok_ref[...].astype(BF16), oht[...])
    low = iota((CHUNK, 128), 1) < 64
    for k in range(N):
        tile = slice(k // 2 * 128, k // 2 * 128 + 128)
        x_k, dy_k = out[0:CHUNK, tile], out[CHUNK : 2 * CHUNK, tile]
        if k % 2 == 0:
            dy_k = pltpu.roll(dy_k, 64, 1)
        else:
            x_k = pltpu.roll(x_k, 64, 1)
        msg[k] = jnp.where(low, x_k, dy_k).astype(BF16)

    pl.semaphore_wait(bar, 2 * (N - 1) + 6)

    def to_expert(j, src, dst, ss, rs):
        return remote(src.at[wrap(e + j)], dst.at[e], ss.at[j], rs.at[j], {"expert": wrap(e + j)})

    a2a = [to_expert(j, msg, blk, a_s, a_r) for j in PEERS]
    for c in a2a:
        c.start()
    blk[e] = msg[e]

    r1 = iota((N * 128, 1), 0)
    blk_i, j_i = r1 // 128, lax.rem(r1, 128)
    is_dy = j_i >= 64
    jj = jnp.where(is_dy, j_i - 64, j_i)
    pos = blk_i * CAP + jj
    lane = jnp.where(pos < MAIN, pos + jnp.where(is_dy, MAIN, 0), pos + jnp.where(is_dy, MAIN + 64, MAIN))
    lane = jnp.where(jj < CAP, lane, -1)
    place[...] = (iota((N * 128, XD), 1) == lane).astype(BF16)

    def placed(k):
        return nn(blk[k], place[pl.ds(pl.multiple_of(k * 128, 128), 128), :])

    chunk = placed(e)
    for j, c in zip(reversed(PEERS), reversed(a2a)):
        c.wait_recv()
        chunk = chunk + placed(wrap(e - j))
    xd[hid] = chunk.astype(BF16)

    def small(k, q, chunk, to):
        h = hx(q, chunk, 0)
        return remote(xd.at[h], xd.at[h], m_s.at[k], m_r.at[k], {"hidden": hx(q, to, 0)})

    def small_recv(k):
        h = hx(k % 2, k, 0)
        remote(xd.at[h], xd.at[h], m_s.at[k], m_r.at[k], {"hidden": hid}).wait_recv()

    def big(q, i, d, s, sel=0):
        to = 1 - 2 * d
        h = chunk_of(q, sel, i, (s + q) % 2, -to * s)
        c, i = way[q], i + sel
        return remote(
            xd.at[h], xd.at[h], g_s.at[c, d, s, i], g_r.at[c, d, s, i], {"hidden": hx(q, 0, to)}
        )

    def big_recv(q, i, d, s, sel=0):
        to = 1 - 2 * d
        h = chunk_of(q, sel, i, (s + 1 + q) % 2, -to * (s + 1))
        c, i = way[q], i + sel
        remote(xd.at[h], xd.at[h], g_s.at[c, d, s, i], g_r.at[c, d, s, i], {"hidden": hid}).wait_recv()

    def goes_far(q, d, s):
        c = side(q, (s + q) % 2)
        return c if d == 0 else 1 - c

    def stays(q, d, s):
        return 1 - goes_far(q, d, s)

    def send_big(q, i, s):
        for d in (0, 1):
            if s > 0:
                big_recv(q, i, d, s - 1)
            big(q, i, d, s).start()

    turn = side(0, 0)
    far = 2 - 4 * turn
    sends = [small(1, 0, 0, -1), small(7, 0, 0, 1), small(2, 0, 0, -2), small(6, 0, 0, 2)]
    relay = [small(3, 0, 2, -1), small(5, 0, -2, 1), small(4, 0, far, -far)]
    sends[0].start()
    sends[1].start()
    send_big(0, 2, 0)
    sends[2].start()
    sends[3].start()
    for c in loads:
        c.wait()
    for k in range(D // 128):
        wdt[pl.ds(k * 128, 128), :] = wd[:, k * 128 : (k + 1) * 128].T
    acc_gu[...] = jnp.zeros_like(acc_gu)
    acc_d[...] = jnp.zeros_like(acc_d)
    acc_t[...] = jnp.zeros_like(acc_t)
    small_recv(1)
    send_big(1, 2, 0)
    small_recv(7)
    send_big(1, 1, 0)
    small_recv(2)
    relay[0].start()
    small_recv(6)
    relay[1].start()
    relay[2].start()
    send_big(0, 3, 0)
    send_big(0, 1, 0)
    small_recv(3)
    send_big(1, 3, 0)
    small_recv(5)
    send_big(1, 0, 0)
    small_recv(4)
    send_big(0, 0, 0)

    def forward(hs):
        left = jnp.concatenate(
            [jnp.concatenate([wg[rows(h), :], wu[rows(h), :], wdt[rows(h), :]], axis=1) for h in hs], axis=0
        )
        right = jnp.concatenate([xd[h] for h in hs], axis=0)
        acc_gu[...] += tn(left[:, 0 : 2 * HID], right[:, 0:MAIN])
        acc_d[...] += tn(left[:, 2 * HID : 3 * HID], right[:, MAIN : 2 * MAIN])
        acc_t[...] += tn(left, right[:, 2 * MAIN : XD])

    def column(dist):
        return [hx(q, off(i, (q + dist) % 2), dist) for q in (0, 1) for i in range(4)]

    forward(column(0))
    for s in range(1, 4):
        if s < 3:
            for pick in (goes_far, stays):
                for j in (1, 0):
                    for q in (0, 1):
                        for d in (0, 1):
                            sel = pick(q, d, s)
                            big_recv(q, 2 * j, d, s - 1, sel)
                            big(q, 2 * j, d, s, sel).start()
        else:
            for j in (0, 1):
                for q in (0, 1):
                    for d in (0, 1):
                        sel = goes_far(q, d, 3)
                        big_recv(q, 2 * j, d, 2, sel)
                        big(q, 2 * j, d, 3, sel).start()
            for q in (0, 1):
                for d in (0, 1):
                    for j in (0, 1):
                        big_recv(q, 2 * j, d, 2, stays(q, d, 3))

        def two(k, carry):
            forward(column((1 - 2 * k) * s))
            return carry

        lax.fori_loop(0, 2, two, 0)

    for q in (0, 1):
        for d in (0, 1):
            for j in (0, 1):
                big_recv(q, 2 * j, d, 3, goes_far(q, d, 4))
    forward(column(4))

    def units(gate, up, dh):
        sig = jax.nn.sigmoid(gate)
        act = gate * sig
        return (
            (act * up).astype(BF16),
            (dh * up * sig * (1.0 + gate * (1.0 - sig))).astype(BF16),
            (dh * act).astype(BF16),
        )

    h_m, g_m, u_m = units(acc_gu[0:HID, :], acc_gu[HID : 2 * HID, :], acc_d[...])
    tail = acc_t[...]
    dh_t = pltpu.roll(tail[2 * HID : 3 * HID, :], 64, 1)
    h_t, g_t, u_t = units(tail[0:HID, :], tail[HID : 2 * HID, :], dh_t)
    low_h = iota((HID, 128), 1) < 64
    for k, (m, t) in enumerate(((g_m, g_t), (u_m, u_t))):
        span = slice(k * HID, (k + 1) * HID)
        t = jnp.where(low_h, t.astype(F32), 0.0)
        gcat[span, 0:MAIN] = m
        gcat[span, MAIN:DR] = t.astype(BF16)
        gcat[span, DR : DR + 128] = pltpu.roll(t, 64, 1).astype(BF16)
    hcat[:, 0:MAIN] = h_m
    hcat[:, MAIN:DR] = pltpu.roll(jnp.where(low_h, h_t.astype(F32), 0.0), 64, 1).astype(BF16)

    def partial_sums(dist):
        hs = column(dist)
        left = jnp.concatenate(
            [jnp.concatenate([wg[rows(h), :], wu[rows(h), :]], axis=1) for h in hs], axis=0
        )
        res = nn(left, gcat[...])
        for n, h in enumerate(hs):
            block = res[n * CHUNK : (n + 1) * CHUNK]
            part[h, :, 0:MAIN] = block[:, 0:MAIN]
            part[h, :, MAIN:DR] = block[:, MAIN:DR] if n % 4 < 2 else block[:, DR : DR + 128]

    def reduce_copy(q, d, short, m, n):
        place = (way[q], d, short, m, n)
        hops = MESSAGES[short][m][1] if isinstance(m, int) else 1
        to = hops * (1 - 2 * d)
        return remote(
            rsend.at[place], rrecv.at[place], r_s.at[place], r_r.at[place], {"hidden": hx(q, 0, to)}
        )

    def pair_parts(q, sel, odd, dist, span):
        h0, h1 = [chunk_of(q, sel, i, odd, dist) for i in (0, 2)]
        return [part[h0, span, 0:MAIN], part[h1, span, 0:MAIN], part[h0, span, MAIN:DR] + part[h1, span, MAIN:DR]]

    def add_message(values, message):
        spans = ((0, MAIN), (MAIN, 2 * MAIN), (2 * MAIN, XD))
        return [v + message[:, lo:hi].astype(F32) for v, (lo, hi) in zip(values, spans)]

    def reduce_step(q, d, short, m, n):
        dist, _, merged = MESSAGES[short][m]
        odd = (q + dist) % 2
        sel = side(q, odd)
        sel = sel if d == short else 1 - sel
        values = pair_parts(q, sel, odd, (1 - 2 * d) * dist, slice(n * PART, (n + 1) * PART))
        c = way[q]
        for k in merged:
            reduce_copy(q, d, short, k, n).wait_recv()
            values = add_message(values, rrecv[c, d, short, k, n])
        rsend[c, d, short, m, n] = jnp.concatenate([v.astype(BF16) for v in values], axis=1)
        reduce_copy(q, d, short, m, n).start()

    def reduce_send(short, m):
        for n in range(CHUNK // PART):
            for q in (0, 1):
                for d in (0, 1):
                    reduce_step(q, d, short, m, n)

    def weight_grads(g):
        span = pl.ds(pl.multiple_of(g * N * CHUNK, N * CHUNK), N * CHUNK)
        feat = xd[pl.ds(g * N, N)].reshape(N * CHUNK, XD)
        x_rows = jnp.concatenate([feat[:, 0:MAIN], feat[:, 2 * MAIN : XD]], axis=1)
        dy_rows = feat[:, MAIN:XD]
        pair = nt(x_rows, gcat[:, 0:DR]).astype(BF16)
        gg[span, :] = pair[:, 0:HID]
        gu[span, :] = pair[:, HID : 2 * HID]
        gd[:, span] = nt(hcat[...], dy_rows).astype(BF16)
        for k, (src, dst) in enumerate(((gg, gg_hbm), (gu, gu_hbm))):
            pltpu.make_async_copy(src.at[span, :], dst.at[span, :], osem.at[k, g]).start()
        pltpu.make_async_copy(gd.at[:, span], gd_hbm.at[:, span], osem.at[2, g]).start()

    def grads(lo, hi):
        def one(g, carry):
            weight_grads(g)
            return carry

        lax.fori_loop(lo, hi, one, 0)

    partial_sums(4)
    reduce_send(0, 0)

    def near(dist):
        def both(k, carry):
            partial_sums((1 - 2 * k) * dist)
            return carry

        lax.fori_loop(0, 2, both, 0)

    near(3)
    reduce_send(1, 0)
    near(2)
    reduce_send(0, 1)
    near(1)
    partial_sums(0)
    reduce_send(0, 2)
    reduce_send(1, 1)
    grads(0, 4)
    reduce_send(0, 3)
    reduce_send(1, 2)
    grads(4, 8)

    def small_sum(k, q):
        return remote(ssend.at[k], srecv.at[k], s_s.at[k], s_r.at[k], {"hidden": hx(q, k, 0)})

    for q, sel in ((0, 0), (1, 0), (1, 1), (0, 1)):
        bit = lax.rem(side(q, q) + sel, 2)
        c = way[q]
        values = pair_parts(q, sel, q, 0, slice(0, CHUNK))
        for d, short in ((0, bit), (1, 1 - bit)):
            last = 3 - short
            for n in range(CHUNK // PART):
                reduce_copy(q, d, short, last, n).wait_recv()
            values = add_message(values, rrecv[c, d, short, last].reshape(CHUNK, XD))
        for j in (0, 1):
            k = off(sel + 2 * j, q) % N
            if k == 0:
                main, high = values[1], values[2]
            else:
                ssend[k] = jnp.concatenate([values[j].astype(BF16), values[2].astype(BF16)], axis=1)
                small_sum(k, q).start()
    for c in a2a:
        c.wait_send()
    for c in sends + relay:
        c.wait_send()
    for q in (0, 1):
        for d in (0, 1):
            for s in range(3):
                for i in range(4):
                    big(q, i, d, s).wait_send()
            for j in (0, 1):
                big(q, 2 * j, d, 3, goes_far(q, d, 3)).wait_send()
            for short in (0, 1):
                for s in range(4 - short):
                    for n in range(CHUNK // PART):
                        reduce_copy(q, d, short, s, n).wait_send()
    low_sum = jnp.zeros((CHUNK, 128), F32)

    p_i = iota((DR, N * 128), 0)
    c_i = iota((DR, N * 128), 1)
    j_c = lax.rem(c_i, 128) - 64 * core
    pick = ((p_i == (c_i // 128) * CAP + j_c) & (j_c >= 0) & (j_c < CAP)).astype(BF16)

    for k in (1, 7, 2, 6, 3, 5, 4):
        remote(ssend.at[k], srecv.at[k], s_s.at[k], s_r.at[k], {"hidden": hid}).wait_recv()
        main = main + srecv[k, :, 0:MAIN].astype(F32)
        if k >= 4:
            low_sum = low_sum + srecv[k, :, MAIN:DR].astype(F32)
        else:
            high = high + srecv[k, :, MAIN:DR].astype(F32)
    tail = low_sum + pltpu.roll(high, 64, 1)
    total = jnp.concatenate([main.astype(BF16), tail.astype(BF16)], axis=1)
    back = nn(total, pick).astype(BF16)
    for k in range(N):
        bsend[k] = back[:, k * 128 : (k + 1) * 128]
    home = [to_expert(j, bsend, brecv, b_s, b_r) for j in PEERS]
    for c in home:
        c.start()
    brecv[e] = bsend[e]

    for k in range(1, N):
        small_sum(k, k % 2).wait_send()
    def flush(g, carry):
        span = pl.ds(pl.multiple_of(g * N * CHUNK, N * CHUNK), N * CHUNK)
        for k, (src, dst) in enumerate(((gg, gg_hbm), (gu, gu_hbm))):
            pltpu.make_async_copy(src.at[span, :], dst.at[span, :], osem.at[k, g]).wait()
        pltpu.make_async_copy(gd.at[:, span], gd_hbm.at[:, span], osem.at[2, g]).wait()
        return carry

    lax.fori_loop(0, N, flush, 0)
    for c in home:
        c.wait()
    cat = jnp.concatenate([jnp.where(low, brecv[k], brecv[k + 1]) for k in range(0, N, 2)], axis=1)
    gt_ref[...] = nn(cat, oht[...]).astype(BF16)


def copy_kernel(gt, gg, gu, gd, gt_out, gg_out, gu_out, gd_out, sem):
    copies = [
        pltpu.make_async_copy(src, dst, sem.at[k])
        for k, (src, dst) in enumerate(((gg, gg_out), (gu, gu_out), (gd, gd_out)))
    ]
    for c in copies:
        c.start()
    gt_out[...] = gt[...]
    for c in copies:
        c.wait()


def local(tokens, grad_out, lang_ids, gate_weight, up_weight, down_weight):
    vmem = pl.BlockSpec(memory_space=pltpu.VMEM)
    anyspace = pl.BlockSpec(memory_space=pl.ANY)
    hbm = pl.BlockSpec(memory_space=pltpu.HBM)
    dma = pltpu.SemaphoreType.DMA
    scratch = [
        pltpu.VMEM((D, HID), BF16),
        pltpu.VMEM((D, HID), BF16),
        pltpu.VMEM((HID, D), BF16),
        pltpu.VMEM((D, HID), BF16),
        pltpu.VMEM((N, CHUNK, 128), BF16),
        pltpu.VMEM((N, CHUNK, 128), BF16),
        pltpu.VMEM((64, CHUNK, XD), BF16),
        pltpu.VMEM((N * 128, XD), BF16),
        pltpu.VMEM((N * 64, 128), BF16),
        pltpu.VMEM((2 * HID, MAIN), F32),
        pltpu.VMEM((HID, MAIN), F32),
        pltpu.VMEM((3 * HID, 128), F32),
        pltpu.VMEM((2 * HID, DR + 128), BF16),
        pltpu.VMEM((HID, DR), BF16),
        pltpu.VMEM((64, CHUNK, DR), F32),
        pltpu.VMEM((2, 2, 2, 4, CHUNK // PART, PART, XD), BF16),
        pltpu.VMEM((2, 2, 2, 4, CHUNK // PART, PART, XD), BF16),
        pltpu.VMEM((N, CHUNK, DR), BF16),
        pltpu.VMEM((N, CHUNK, DR), BF16),
        pltpu.VMEM((N, CHUNK, 128), BF16),
        pltpu.VMEM((N, CHUNK, 128), BF16),
        pltpu.VMEM((D, HID), BF16),
        pltpu.VMEM((D, HID), BF16),
        pltpu.VMEM((HID, D), BF16),
        dma((3,)),
        dma((N,)), dma((N,)),
        dma((N,)), dma((N,)),
        dma((2, 2, 4, 4)), dma((2, 2, 4, 4)),
        dma((2, 2, 2, 4, CHUNK // PART)), dma((2, 2, 2, 4, CHUNK // PART)),
        dma((N,)), dma((N,)),
        dma((N,)), dma((N,)),
        dma((3, N)),
    ]
    packed = jnp.concatenate([v.T.astype(F32) for v in (tokens, grad_out)], axis=0)
    shapes = (
        jax.ShapeDtypeStruct((CHUNK, 128), BF16),
        jax.ShapeDtypeStruct((D, HID), BF16),
        jax.ShapeDtypeStruct((D, HID), BF16),
        jax.ShapeDtypeStruct((HID, D), BF16),
    )
    out = pl.pallas_call(
        kernel,
        out_shape=shapes,
        in_specs=[vmem] * 2 + [hbm] * 3,
        out_specs=(vmem, anyspace, anyspace, anyspace),
        scratch_shapes=scratch,
        compiler_params=pltpu.CompilerParams(
            collective_id=0, has_side_effects=True, vmem_limit_bytes=103 * 512 * 1024
        ),
        cost_estimate=pl.CostEstimate(
            flops=16 * 320 * D * HID, bytes_accessed=6 * D * HID * 2, transcendentals=320 * HID
        ),
    )(
        packed, lang_ids.T, gate_weight[0], up_weight[0], down_weight[0]
    )
    out = pl.pallas_call(
        copy_kernel,
        out_shape=shapes,
        in_specs=[vmem, anyspace, anyspace, anyspace],
        out_specs=(vmem, hbm, hbm, hbm),
        scratch_shapes=[dma((3,))],
        compiler_params=pltpu.CompilerParams(vmem_limit_bytes=8 * 1024 * 1024),
    )(*out)
    return out[0].T, out[1][None], out[2][None], out[3][None]


def solution(mesh):
    in_specs = (
        P("expert", "hidden"),
        P("expert", "hidden"),
        P("expert", None),
        P("expert", None, "hidden"),
        P("expert", None, "hidden"),
        P("expert", "hidden", None),
    )
    out_specs = (
        P("expert", "hidden"),
        P("expert", None, "hidden"),
        P("expert", None, "hidden"),
        P("expert", "hidden", None),
    )
    return jax.shard_map(local, mesh=mesh, in_specs=in_specs, out_specs=out_specs, check_vma=False)
```
